256 devices in a mesh: sub: 2 (over core), row: 8 (over y_lo, x), col: 16 (over z, y_hi).
Axes of the slice: x: 4, y: 4 (y_hi: 2, y_lo: 2; y = y_hi * 2 + y_lo), z: 8, core: 2. Of those that a mesh axis runs over, the one named last changes fastest.
Arguments:
- initial: float32 [12, 16, 256, 4096], P(None, ('sub', 'row'), None, 'col'), may hold values from -1 to 6
- pattern: int32 [12, 16, 16], P(None, ('sub', 'row'), 'col'), may hold values from 0 to 1, as said below
- rmap: int32 [2, 8, 16], replicated, may hold values from 0 to 191, as said below
- child_update: float32 [2, 8, 16, 256, 4096], P('sub', 'row', None, None, 'col'), may hold values from -0.5 to 0.5
Outputs:
- factored: float32 [12, 16, 256, 4096], P(None, ('sub', 'row'), None, 'col')
The draws below stay inside these ranges and needn't reach their ends.
Inputs may be any that keep to these rules, and one draw needn't show every extreme that they name: Within one child the 128 entries are distinct tile rows; in each block rmap[c, r, :] exactly two remainders modulo 16 appear 2 times, two never, the others once. pattern[p, p] = 1 for p < 16.
All inputs are finite; a program needn't handle non-finite values.
Results may differ from the reference program's by a relative error of at most 0.0001.
Values sent between devices are 32-bit elements; how exact they have to be, the bound alone decides.
A program may use at most 128 MiB of HBM per device.

```python
import jax
import jax.numpy as jnp
from jax import lax

TB = 256
FTL = 12
OWNERS = 16
CHILDREN = 2
CHILD_ROWS = 8
WINDOW = 16


def child_table(child_key):
    key_dest, key_order, key_slot = jax.random.split(child_key, 3)
    perm_dest = jax.random.permutation(key_dest, OWNERS)
    base = jnp.broadcast_to(jnp.arange(OWNERS)[None, :], (CHILD_ROWS, OWNERS))
    proc_row = jnp.arange(CHILD_ROWS)[:, None]
    offset = (base - 2 * proc_row) % OWNERS
    picked = jnp.where((offset == 2) | (offset == 3), (base - 2) % OWNERS, base)
    dest = perm_dest[picked]
    orders = jax.vmap(lambda kk: jax.random.permutation(kk, OWNERS))(jax.random.split(key_order, CHILD_ROWS))
    dest = jnp.take_along_axis(dest, orders, axis=1)
    flat = dest.reshape(-1)
    index = jnp.arange(flat.shape[0])
    ranks = jnp.sum(((flat[None, :] == flat[:, None]) & (index[None, :] < index[:, None])).astype(jnp.int32), axis=1)
    slot_perm = jax.vmap(lambda kk: jax.random.permutation(kk, FTL))(jax.random.split(key_slot, OWNERS))
    local = slot_perm[flat, ranks]
    return (local * OWNERS + flat).reshape(CHILD_ROWS, OWNERS).astype(jnp.int32)


def map_table(key):
    tables = [child_table(jax.random.fold_in(key, 100 + c)) for c in range(CHILDREN)]
    return jnp.stack(tables, axis=0)


def draw_rmap(key, part):
    return map_table(jax.random.fold_in(key, 11))


def draw_pattern(key, part):
    bits = jax.random.randint(jax.random.fold_in(key, 13), (FTL, OWNERS, WINDOW), 0, 2)
    tile_row = jnp.arange(FTL)[:, None, None] * OWNERS + jnp.arange(OWNERS)[None, :, None]
    tile_col = jnp.arange(WINDOW)[None, None, :]
    return jnp.where(tile_row == tile_col, 1, bits).astype(jnp.int32)


def draw_initial(key, part):
    width = WINDOW * TB
    key_val = jax.random.fold_in(jax.random.fold_in(key, 14), 0)
    values = jax.random.uniform(key_val, (FTL, OWNERS, TB, width), jnp.float32, -1.0, 1.0)
    tile_row = jnp.arange(FTL)[:, None, None, None] * OWNERS + jnp.arange(OWNERS)[None, :, None, None]
    scale = jnp.where(tile_row < 2, 1.0 / TB, 1.0)
    in_row = jnp.arange(TB)[None, None, :, None]
    column = jnp.arange(width)[None, None, None, :]
    diagonal = (tile_row == column // TB) & (in_row == column % TB)
    return (values * scale + jnp.where(diagonal, 5.0, 0.0)).astype(jnp.float32)


def draw_child_update(key, part):
    width = WINDOW * TB
    maps = map_table(jax.random.fold_in(key, 11))
    key_val = jax.random.fold_in(jax.random.fold_in(key, 12), 0)
    values = jax.random.uniform(key_val, (CHILDREN, CHILD_ROWS, OWNERS, TB, width), jnp.float32, -1.0, 1.0)
    lead = (maps < 2)[:, :, :, None, None]
    scale = jnp.where(lead, 0.5 / TB, 0.5)
    return (values * scale).astype(jnp.float32)


def setup_inputs(seed: int = 0) -> dict:
    key_of = jax.random.split(jax.random.key(seed), 5)
    initial = draw_initial(jax.random.fold_in(key_of[4], 71), 0)
    pattern = draw_pattern(jax.random.fold_in(key_of[4], 71), 0)
    rmap = draw_rmap(jax.random.fold_in(key_of[4], 71), 0)
    child_update = draw_child_update(jax.random.fold_in(key_of[4], 71), 0)
    return dict(initial=initial, pattern=pattern, rmap=rmap, child_update=child_update)


def reference(initial, pattern, rmap, child_update):
    total_rows = FTL * OWNERS
    width = WINDOW * TB
    mask = jnp.repeat(pattern.reshape(total_rows, WINDOW).astype(jnp.float32), TB, axis=1)
    front = initial.reshape(total_rows, TB, width) * mask[:, None, :]
    front = front.at[rmap.reshape(-1)].add(child_update.reshape(-1, TB, width))
    rows = jnp.arange(total_rows)
    col_tile = jnp.arange(width) // TB
    for k in range(2):
        factor = jnp.linalg.cholesky(front[k, :, k * TB:(k + 1) * TB])
        column = front[:, :, k * TB:(k + 1) * TB]
        solved = lax.linalg.triangular_solve(factor, column.reshape(-1, TB), left_side=False, lower=True, transpose_a=True)
        solved = solved.reshape(total_rows, TB, TB)
        panel = jnp.where((rows == k)[:, None, None], factor[None], jnp.where((rows > k)[:, None, None], solved, jnp.zeros_like(solved)))
        top = panel[:WINDOW]
        update = jnp.einsum('pab,jcb->pajc', panel, top, precision=lax.Precision.HIGHEST).reshape(total_rows, TB, width)
        keep = (col_tile > k)[None, None, :] & (rows > k)[:, None, None]
        front = jnp.where(keep, front - update, front)
        front = front.at[:, :, k * TB:(k + 1) * TB].set(panel)
    return front.reshape(FTL, OWNERS, TB, width)
```

```python
import functools

import jax
import jax.numpy as jnp
from jax import lax
from jax.experimental import pallas as pl
from jax.experimental.pallas import tpu as pltpu
from jax.sharding import PartitionSpec as P

MESH = pl.DeviceIdType.MESH
MIB = 1024 * 1024
HIGHEST = lax.Precision.HIGHEST


def tables(rmap, owner_me, frows):
    owners = rmap.shape[2]
    maps = rmap.reshape(-1, owners)
    target = maps % owners
    index = jnp.arange(owners)
    earlier = (target[:, None, :] == target[:, :, None]) & (index[None, None, :] < index[None, :, None])
    rank = jnp.sum(earlier.astype(jnp.int32), axis=2)
    mine = jnp.sum(jnp.where((index == owner_me)[:, None], target, 0), axis=0)
    mine_rank = jnp.sum(jnp.where((index == owner_me)[:, None], rank, 0), axis=0)
    dest = index ^ owner_me
    hit = (mine[None, None, :] == dest[:, None, None]) & (mine_rank[None, None, :] == jnp.arange(2)[None, :, None])
    send = jnp.sum(jnp.where(hit, index[None, None, :], 0), axis=2).reshape(-1)
    place = (index ^ owner_me)[:, None] * 2 + rank
    wanted = jnp.arange(frows) * owners + owner_me
    found = maps.reshape(2, -1)[None] == wanted[:, None, None]
    look = jnp.sum(jnp.where(found, place.reshape(2, -1)[None], 0), axis=2)
    here = jnp.sum(found.astype(jnp.int32), axis=2)
    return send.astype(jnp.int32), look.reshape(-1).astype(jnp.int32), here.reshape(-1).astype(jnp.int32)


def exchange_kernel(
    send_ref, look_ref, here_ref, pattern_ref, initial_ref, child_ref,
    front_ref, cols_ref, lead_ref,
    out_buf, in_buf,
    x_send, x_recv, a_send, a_recv, c_send, c_recv, b_send, b_recv, s_send, s_recv, g_send, g_recv,
):
    rows = lax.axis_size("row")
    owners = lax.axis_size("sub") * rows
    depth = lax.axis_size("col") // 2
    frows, tile = initial_ref.shape[0], initial_ref.shape[2]
    half = tile // 2
    sub, row, col = lax.axis_index("sub"), lax.axis_index("row"), lax.axis_index("col")
    me = sub * rows + row
    z, plane = col // 2, col % 2
    other = 1 - plane

    def peer(delta):
        there = me ^ delta
        return (there // rows, there % rows, col)

    up = (sub, row, ((z + 1) % depth) * 2 + plane)
    down = (sub, row, ((z + depth - 1) % depth) * 2 + plane)
    across = (sub, row, z * 2 + other)
    ways = (up, down)

    barrier = pltpu.get_barrier_semaphore()
    for delta in range(1, owners):
        pl.semaphore_signal(barrier, inc=1, device_id=peer(delta), device_id_type=MESH)
    for there in (up, down, across):
        pl.semaphore_signal(barrier, inc=1, device_id=there, device_id_type=MESH)

    for s in range(2):
        out_buf[s] = child_ref[0, 0, send_ref[s]]

    def fill(delta, carry):
        for s in range(2):
            out_buf[delta * 2 + s] = child_ref[0, 0, send_ref[delta * 2 + s]]
        return carry

    lax.fori_loop(1, owners, fill, 0)
    for s in range(2):
        in_buf[s] = out_buf[s]
    pl.semaphore_wait(barrier, owners - 1 + 3)

    def x_copy(delta):
        part = pl.ds(delta * 2, 2)
        return pltpu.make_async_remote_copy(
            src_ref=out_buf.at[part], dst_ref=in_buf.at[part], send_sem=x_send.at[delta],
            recv_sem=x_recv.at[delta], device_id=peer(delta), device_id_type=MESH,
        )

    for delta in range(1, owners):
        x_copy(delta).start()
    for delta in range(1, owners):
        x_copy(delta).wait_recv()

    def assemble(m, carry):
        value = initial_ref[m, 0] * pattern_ref[m].astype(jnp.float32)
        for c in range(2):
            tile_in = in_buf[look_ref[m * 2 + c]]
            value = value + jnp.where(here_ref[m * 2 + c] > 0, tile_in, 0.0)
        front_ref[m] = value

        @pl.when(z == 0)
        def _():
            cols_ref[plane, m] = value

        return carry

    lax.fori_loop(0, frows, assemble, 0)

    quarter = half // 2

    def a_copy(h, i):
        part = cols_ref.at[plane, i // 2, pl.ds(h * half + (i % 2) * quarter, quarter)]
        return pltpu.make_async_remote_copy(
            src_ref=part, dst_ref=part, send_sem=a_send.at[h, i], recv_sem=a_recv.at[h, i],
            device_id=ways[h], device_id_type=MESH,
        )

    passes_on = (z != depth - 1, z != 1)

    def a_step(i, carry):
        for h in range(2):
            @pl.when(z != 0)
            def _():
                a_copy(h, i).wait_recv()

            @pl.when(passes_on[h])
            def _():
                a_copy(h, i).start()

        return carry

    lax.fori_loop(0, 2 * frows, a_step, 0)

    piece = half // depth
    group = frows // 2

    def cut(k, h, g, origin):
        return cols_ref.at[k, pl.ds(g * group, group), pl.ds(h * half + origin * piece, piece)]

    def c_copy(k, h, g):
        part = cut(k, h, g, z)
        return pltpu.make_async_remote_copy(
            src_ref=part, dst_ref=part, send_sem=c_send.at[h, g], recv_sem=c_recv.at[h, g],
            device_id=across, device_id_type=MESH,
        )

    for g in range(2):
        for h in range(2):
            c_copy(plane, h, g).start()

    def b_copy(h, g, t, origin):
        part = cut(other, h, g, origin)
        return pltpu.make_async_remote_copy(
            src_ref=part, dst_ref=part, send_sem=b_send.at[h, g, t], recv_sem=b_recv.at[h, g, t],
            device_id=ways[h], device_id_type=MESH,
        )

    def origin_of(h, t):
        return (z + depth - t) % depth if h == 0 else (z + t) % depth

    for g in range(2):
        for h in range(2):
            c_copy(other, h, g).wait_recv()
            b_copy(h, g, 0, origin_of(h, 0)).start()

    def b_step(t, carry):
        for g in range(2):
            for h in range(2):
                b_copy(h, g, t - 1, origin_of(h, t)).wait_recv()

                @pl.when(t < depth - 1)
                def _():
                    b_copy(h, g, t, origin_of(h, t)).start()

        return carry

    lax.fori_loop(1, depth, b_step, 0)

    strip = tile // owners
    sources = (0, 1, col % owners)

    def s_copy(s, delta):
        rows_there = pl.ds((me ^ delta) * strip, strip)
        return pltpu.make_async_remote_copy(
            src_ref=cols_ref.at[:, 0, rows_there], dst_ref=lead_ref.at[s, :, rows_there],
            send_sem=s_send.at[s, delta], recv_sem=s_recv.at[s], device_id=peer(delta), device_id_type=MESH,
        )

    for s, source in enumerate(sources):
        @pl.when(me == source)
        def _():
            for delta in range(1, owners):
                s_copy(s, delta).start()
            mine = pl.ds(pl.multiple_of(me * strip, strip), strip)
            lead_ref[s, :, mine] = cols_ref[:, 0, mine]

    def s_arrival(s):
        mine = pl.ds(me * strip, strip)
        return pltpu.make_async_remote_copy(
            src_ref=cols_ref.at[:, 0, mine], dst_ref=lead_ref.at[s, :, mine],
            send_sem=s_send.at[s, 0], recv_sem=s_recv.at[s], device_id=across, device_id_type=MESH,
        )

    for s, source in enumerate(sources):
        @pl.when(me != source)
        def _():
            s_arrival(s).wait_recv()

    def g_copy(delta, holder):
        part = lead_ref.at[:, :, pl.ds(holder * strip, strip)]
        return pltpu.make_async_remote_copy(
            src_ref=part, dst_ref=part, send_sem=g_send.at[delta], recv_sem=g_recv.at[delta],
            device_id=peer(delta), device_id_type=MESH,
        )

    for delta in range(1, owners):
        g_copy(delta, me).start()
    for delta in range(1, owners):
        g_copy(delta, me ^ delta).wait_recv()

    for delta in range(1, owners):
        g_copy(delta, me).wait_send()
        x_copy(delta).wait_send()
    for s, source in enumerate(sources):
        @pl.when(me == source)
        def _():
            for delta in range(1, owners):
                s_copy(s, delta).wait_send()
    for g in range(2):
        for h in range(2):
            c_copy(plane, h, g).wait_send()

    def b_end(t, carry):
        for g in range(2):
            for h in range(2):
                b_copy(h, g, t, origin_of(h, t)).wait_send()
        return carry

    lax.fori_loop(0, depth - 1, b_end, 0)

    def a_end(i, carry):
        for h in range(2):
            @pl.when(passes_on[h])
            def _():
                a_copy(h, i).wait_send()
        return carry

    lax.fori_loop(0, 2 * frows, a_end, 0)


def exchange(initial, pattern, rmap, child_update):
    owners = lax.axis_size("sub") * lax.axis_size("row")
    depth = lax.axis_size("col") // 2
    frows, _, tile, _ = initial.shape
    me = lax.axis_index(("sub", "row"))
    send, look, here = tables(rmap, me, frows)
    smem = pl.BlockSpec(memory_space=pltpu.SMEM)
    vmem = pl.BlockSpec(memory_space=pltpu.VMEM)
    dma = pltpu.SemaphoreType.DMA
    return pl.pallas_call(
        exchange_kernel,
        out_shape=(
            jax.ShapeDtypeStruct((frows, tile, tile), jnp.float32),
            jax.ShapeDtypeStruct((2, frows, tile, tile), jnp.float32),
            jax.ShapeDtypeStruct((3, 2, tile, tile), jnp.float32),
        ),
        in_specs=[smem] * 4 + [vmem] * 2,
        out_specs=(vmem, vmem, vmem),
        scratch_shapes=[
            pltpu.VMEM((2 * owners, tile, tile), jnp.float32),
            pltpu.VMEM((2 * owners, tile, tile), jnp.float32),
            dma((owners,)), dma((owners,)),
            dma((2, 2 * frows)), dma((2, 2 * frows)),
            dma((2, 2)), dma((2, 2)),
            dma((2, 2, depth)), dma((2, 2, depth)),
            dma((3, owners)), dma((3,)),
            dma((owners,)), dma((owners,)),
        ],
        compiler_params=pltpu.CompilerParams(
            collective_id=0, has_side_effects=True, vmem_limit_bytes=56 * MIB
        ),
    )(send, look, here, pattern.reshape(-1), initial, child_update)


def mul(a, b):
    return jnp.dot(a, b, preferred_element_type=jnp.float32, precision=HIGHEST)


def mul_t(a, b):
    return lax.dot_general(
        a, b, (((1,), (1,)), ((), ())), preferred_element_type=jnp.float32, precision=HIGHEST
    )


def factor_block(block):
    n = block.shape[0]
    row_id = lax.broadcasted_iota(jnp.int32, (n, 1), 0)
    eye = (lax.broadcasted_iota(jnp.int32, (n, n), 0) == lax.broadcasted_iota(jnp.int32, (n, n), 1))

    def body(step, carry):
        left, right = carry
        live = row_id < n - 8 * step
        for i in range(8):
            scale = jnp.where((row_id > i) & live, left[:, i:i + 1] / left[i:i + 1, i:i + 1], 0.0)
            left, right = left - scale * left[i:i + 1, :], right - scale * right[i:i + 1, :]
        left = jnp.concatenate([left[8:], left[:8]], axis=0)
        left = pltpu.roll(left, n - 8, 1)
        right = jnp.concatenate([right[8:], right[:8]], axis=0)
        return left, right

    upper, inverse = lax.fori_loop(0, n // 8, body, (block, eye.astype(jnp.float32)))
    scale = lax.rsqrt(jnp.sum(jnp.where(eye, upper, 0.0), axis=1, keepdims=True))
    keep = lax.broadcasted_iota(jnp.int32, (n, n), 0) <= lax.broadcasted_iota(jnp.int32, (n, n), 1)
    return jnp.where(keep, upper * scale, 0.0).T, inverse * scale


def factor_tile(tile_value, factor_ref, inverse_ref):
    n = tile_value.shape[0]
    h = n // 2
    sym = 0.5 * (tile_value + tile_value.T)
    l0, t0 = factor_block(sym[:h, :h])
    l10 = mul_t(sym[h:, :h], t0)
    l1, t1 = factor_block(sym[h:, h:] - mul_t(l10, l10))
    zero = jnp.zeros((h, h), jnp.float32)
    factor_ref[:h, :h] = l0
    factor_ref[:h, h:] = zero
    factor_ref[h:, :h] = l10
    factor_ref[h:, h:] = l1
    inverse_ref[:h, :h] = t0
    inverse_ref[:h, h:] = zero
    inverse_ref[h:, :h] = -mul(t1, mul(l10, t0))
    inverse_ref[h:, h:] = t1


def split(x):
    high = x.astype(jnp.bfloat16)
    return high, (x - high.astype(jnp.float32)).astype(jnp.bfloat16)


def finish_kernel(front_ref, cols_ref, lead_ref, out_ref, f0_ref, i0_ref, f1_ref, i1_ref, own_ref):
    rows = lax.axis_size("row")
    frows, tile = front_ref.shape[0], front_ref.shape[1]
    me = lax.axis_index("sub") * rows + lax.axis_index("row")
    col = lax.axis_index("col")
    eye = (
        lax.broadcasted_iota(jnp.int32, (tile, tile), 0) == lax.broadcasted_iota(jnp.int32, (tile, tile), 1)
    ).astype(jnp.float32)

    factor_tile(lead_ref[0, 0], f0_ref, i0_ref)
    i0 = i0_ref[...]
    l10 = mul_t(lead_ref[1, 0], i0)
    factor_tile(lead_ref[1, 1] - mul_t(l10, l10), f1_ref, i1_ref)
    i1 = i1_ref[...]
    p0 = mul_t(lead_ref[2, 0], i0)
    own_ref[...] = p0
    p1 = mul_t(lead_ref[2, 1] - mul_t(p0, l10), i1)
    p0 = jnp.where(col == 0, eye, jnp.where(col == 1, 0.0, p0))
    p1 = jnp.where(col == 0, 0.0, jnp.where(col == 1, eye, p1))
    n1 = mul(p1, i1)
    n0 = mul(p0 - mul(n1, l10), i0)
    sign = jnp.where(col < 2, 1.0, -1.0)
    keep = jnp.where(col < 2, 0.0, 1.0)
    n0_high, n0_low = split(n0)
    n1_high, n1_low = split(n1)

    def dot_t(a, b):
        return lax.dot_general(a, b, (((1,), (1,)), ((), ())), preferred_element_type=jnp.float32)

    def body(m, carry):
        a0_high, a0_low = split(cols_ref[0, m])
        a1_high, a1_low = split(cols_ref[1, m])
        total = dot_t(a0_low, n0_high) + dot_t(a0_high, n0_low) + dot_t(a1_low, n1_high) + dot_t(a1_high, n1_low)
        total = total + dot_t(a0_high, n0_high) + dot_t(a1_high, n1_high)
        out_ref[m] = keep * front_ref[m] + sign * total
        return carry

    lax.fori_loop(0, frows, body, 0)

    @pl.when(me == 0)
    def _():
        out_ref[0] = jnp.where(col == 0, f0_ref[...], jnp.where(col == 1, 0.0, front_ref[0]))

    @pl.when((me == 1) & (col == 1))
    def _():
        out_ref[0] = f1_ref[...]

    @pl.when((me == 1) & (col > 1))
    def _():
        out_ref[0] = front_ref[0] - mul_t(mul_t(lead_ref[1, 0], i0_ref[...]), own_ref[...])


def finish(front, cols, lead):
    frows, tile, _ = front.shape
    vmem = pl.BlockSpec(memory_space=pltpu.VMEM)
    return pl.pallas_call(
        finish_kernel,
        out_shape=jax.ShapeDtypeStruct(front.shape, jnp.float32),
        in_specs=[vmem] * 3,
        out_specs=vmem,
        scratch_shapes=[pltpu.VMEM((tile, tile), jnp.float32)] * 5,
        compiler_params=pltpu.CompilerParams(vmem_limit_bytes=48 * MIB),
    )(front, cols, lead)


def per_device(initial, pattern, rmap, child_update):
    front, cols, lead = exchange(initial, pattern, rmap, child_update)
    return finish(front, cols, lead)[:, None]


def solution(mesh):
    return jax.shard_map(
        per_device,
        mesh=mesh,
        in_specs=(
            P(None, ("sub", "row"), None, "col"),
            P(None, ("sub", "row"), "col"),
            P(),
            P("sub", "row", None, None, "col"),
        ),
        out_specs=P(None, ("sub", "row"), None, "col"),
        check_vma=False,
    )
```

```python
import functools

import jax
import jax.numpy as jnp
from jax import lax
from jax.experimental import pallas as pl
from jax.experimental.pallas import tpu as pltpu
from jax.sharding import PartitionSpec as P

MESH = pl.DeviceIdType.MESH
MIB = 1024 * 1024
HIGHEST = lax.Precision.HIGHEST


def tables(rmap, owner_me, frows):
    owners = rmap.shape[2]
    maps = rmap.reshape(-1, owners)
    target = maps % owners
    index = jnp.arange(owners)
    earlier = (target[:, None, :] == target[:, :, None]) & (index[None, None, :] < index[None, :, None])
    rank = jnp.sum(earlier.astype(jnp.int32), axis=2)
    mine = jnp.sum(jnp.where((index == owner_me)[:, None], target, 0), axis=0)
    mine_rank = jnp.sum(jnp.where((index == owner_me)[:, None], rank, 0), axis=0)
    dest = index ^ owner_me
    hit = (mine[None, None, :] == dest[:, None, None]) & (mine_rank[None, None, :] == jnp.arange(2)[None, :, None])
    send = jnp.sum(jnp.where(hit, index[None, None, :], 0), axis=2).reshape(-1)
    place = (index ^ owner_me)[:, None] * 2 + rank
    wanted = jnp.arange(frows) * owners + owner_me
    found = maps.reshape(2, -1)[None] == wanted[:, None, None]
    look = jnp.sum(jnp.where(found, place.reshape(2, -1)[None], 0), axis=2)
    here = jnp.sum(found.astype(jnp.int32), axis=2)
    return send.astype(jnp.int32), look.reshape(-1).astype(jnp.int32), here.reshape(-1).astype(jnp.int32)


def exchange_kernel(
    send_ref, look_ref, here_ref, pattern_ref, initial_ref, child_ref,
    front_ref, cols_ref, lead_ref,
    out_buf, in_buf,
    x_send, x_recv, a_send, a_recv, c_send, c_recv, b_send, b_recv, s_send, s_recv, g_send, g_recv,
):
    rows = lax.axis_size("row")
    owners = lax.axis_size("sub") * rows
    depth = lax.axis_size("col") // 2
    frows, tile = initial_ref.shape[0], initial_ref.shape[2]
    half = tile // 2
    sub, row, col = lax.axis_index("sub"), lax.axis_index("row"), lax.axis_index("col")
    me = sub * rows + row
    z, plane = col // 2, col % 2
    other = 1 - plane

    def peer(delta):
        there = me ^ delta
        return (there // rows, there % rows, col)

    up = (sub, row, ((z + 1) % depth) * 2 + plane)
    down = (sub, row, ((z + depth - 1) % depth) * 2 + plane)
    across = (sub, row, z * 2 + other)
    ways = (up, down)

    barrier = pltpu.get_barrier_semaphore()
    for delta in range(1, owners):
        pl.semaphore_signal(barrier, inc=1, device_id=peer(delta), device_id_type=MESH)
    for there in (up, down, across):
        pl.semaphore_signal(barrier, inc=1, device_id=there, device_id_type=MESH)

    for s in range(2):
        out_buf[s] = child_ref[0, 0, send_ref[s]]

    def fill(delta, carry):
        for s in range(2):
            out_buf[delta * 2 + s] = child_ref[0, 0, send_ref[delta * 2 + s]]
        return carry

    lax.fori_loop(1, owners, fill, 0)
    for s in range(2):
        in_buf[s] = out_buf[s]
    pl.semaphore_wait(barrier, owners - 1 + 3)

    def x_copy(delta):
        part = pl.ds(delta * 2, 2)
        return pltpu.make_async_remote_copy(
            src_ref=out_buf.at[part], dst_ref=in_buf.at[part], send_sem=x_send.at[delta],
            recv_sem=x_recv.at[delta], device_id=peer(delta), device_id_type=MESH,
        )

    for delta in range(1, owners):
        x_copy(delta).start()
    for delta in range(1, owners):
        x_copy(delta).wait_recv()

    def assemble(m, carry):
        value = initial_ref[m, 0] * pattern_ref[m].astype(jnp.float32)
        for c in range(2):
            tile_in = in_buf[look_ref[m * 2 + c]]
            value = value + jnp.where(here_ref[m * 2 + c] > 0, tile_in, 0.0)
        front_ref[m] = value

        @pl.when(z == 0)
        def _():
            cols_ref[plane, m] = value

        return carry

    lax.fori_loop(0, frows, assemble, 0)

    quarter = half // 2

    def a_copy(h, i):
        part = cols_ref.at[plane, i // 2, pl.ds(h * half + (i % 2) * quarter, quarter)]
        return pltpu.make_async_remote_copy(
            src_ref=part, dst_ref=part, send_sem=a_send.at[h, i], recv_sem=a_recv.at[h, i],
            device_id=ways[h], device_id_type=MESH,
        )

    hops = (z, (depth - z) % depth)

    def a_step(step, carry):
        for h in range(2):
            i = step - hops[h]
            live = (i >= 0) & (i < 2 * frows)

            @pl.when(live & (z != 0))
            def _():
                a_copy(h, i).wait_recv()

            @pl.when(live & (hops[h] != depth - 1))
            def _():
                a_copy(h, i).start()

        return carry

    lax.fori_loop(0, 2 * frows + depth - 1, a_step, 0)

    piece = half // depth
    group = frows // 2

    def cut(k, h, g, origin):
        return cols_ref.at[k, pl.ds(g * group, group), pl.ds(h * half + origin * piece, piece)]

    def c_copy(k, h, g):
        part = cut(k, h, g, z)
        return pltpu.make_async_remote_copy(
            src_ref=part, dst_ref=part, send_sem=c_send.at[h, g], recv_sem=c_recv.at[h, g],
            device_id=across, device_id_type=MESH,
        )

    for g in range(2):
        for h in range(2):
            c_copy(plane, h, g).start()

    def b_copy(h, g, t, origin):
        part = cut(other, h, g, origin)
        return pltpu.make_async_remote_copy(
            src_ref=part, dst_ref=part, send_sem=b_send.at[h, g, t], recv_sem=b_recv.at[h, g, t],
            device_id=ways[h], device_id_type=MESH,
        )

    def origin_of(h, t):
        return (z + depth - t) % depth if h == 0 else (z + t) % depth

    for g in range(2):
        for h in range(2):
            c_copy(other, h, g).wait_recv()
            b_copy(h, g, 0, origin_of(h, 0)).start()

    def b_step(t, carry):
        for g in range(2):
            for h in range(2):
                b_copy(h, g, t - 1, origin_of(h, t)).wait_recv()

                @pl.when(t < depth - 1)
                def _():
                    b_copy(h, g, t, origin_of(h, t)).start()

        return carry

    lax.fori_loop(1, depth, b_step, 0)

    strip = tile // owners
    sources = (0, 1, col % owners)

    def s_copy(s, delta):
        rows_there = pl.ds((me ^ delta) * strip, strip)
        return pltpu.make_async_remote_copy(
            src_ref=cols_ref.at[:, 0, rows_there], dst_ref=lead_ref.at[s, :, rows_there],
            send_sem=s_send.at[s, delta], recv_sem=s_recv.at[s], device_id=peer(delta), device_id_type=MESH,
        )

    for s, source in enumerate(sources):
        @pl.when(me == source)
        def _():
            for delta in range(1, owners):
                s_copy(s, delta).start()
            mine = pl.ds(pl.multiple_of(me * strip, strip), strip)
            lead_ref[s, :, mine] = cols_ref[:, 0, mine]

    def s_arrival(s):
        mine = pl.ds(me * strip, strip)
        return pltpu.make_async_remote_copy(
            src_ref=cols_ref.at[:, 0, mine], dst_ref=lead_ref.at[s, :, mine],
            send_sem=s_send.at[s, 0], recv_sem=s_recv.at[s], device_id=across, device_id_type=MESH,
        )

    for s, source in enumerate(sources):
        @pl.when(me != source)
        def _():
            s_arrival(s).wait_recv()

    def g_copy(delta, holder):
        part = lead_ref.at[:, :, pl.ds(holder * strip, strip)]
        return pltpu.make_async_remote_copy(
            src_ref=part, dst_ref=part, send_sem=g_send.at[delta], recv_sem=g_recv.at[delta],
            device_id=peer(delta), device_id_type=MESH,
        )

    for delta in range(1, owners):
        g_copy(delta, me).start()
    for delta in range(1, owners):
        g_copy(delta, me ^ delta).wait_recv()

    for delta in range(1, owners):
        g_copy(delta, me).wait_send()
        x_copy(delta).wait_send()
    for s, source in enumerate(sources):
        @pl.when(me == source)
        def _():
            for delta in range(1, owners):
                s_copy(s, delta).wait_send()
    for g in range(2):
        for h in range(2):
            c_copy(plane, h, g).wait_send()

    def b_end(t, carry):
        for g in range(2):
            for h in range(2):
                b_copy(h, g, t, origin_of(h, t)).wait_send()
        return carry

    lax.fori_loop(0, depth - 1, b_end, 0)

    def a_end(i, carry):
        for h in range(2):
            @pl.when(hops[h] != depth - 1)
            def _():
                a_copy(h, i).wait_send()
        return carry

    lax.fori_loop(0, 2 * frows, a_end, 0)


def exchange(initial, pattern, rmap, child_update):
    owners = lax.axis_size("sub") * lax.axis_size("row")
    depth = lax.axis_size("col") // 2
    frows, _, tile, _ = initial.shape
    me = lax.axis_index(("sub", "row"))
    send, look, here = tables(rmap, me, frows)
    smem = pl.BlockSpec(memory_space=pltpu.SMEM)
    vmem = pl.BlockSpec(memory_space=pltpu.VMEM)
    dma = pltpu.SemaphoreType.DMA
    return pl.pallas_call(
        exchange_kernel,
        out_shape=(
            jax.ShapeDtypeStruct((frows, tile, tile), jnp.float32),
            jax.ShapeDtypeStruct((2, frows, tile, tile), jnp.float32),
            jax.ShapeDtypeStruct((3, 2, tile, tile), jnp.float32),
        ),
        in_specs=[smem] * 4 + [vmem] * 2,
        out_specs=(vmem, vmem, vmem),
        scratch_shapes=[
            pltpu.VMEM((2 * owners, tile, tile), jnp.float32),
            pltpu.VMEM((2 * owners, tile, tile), jnp.float32),
            dma((owners,)), dma((owners,)),
            dma((2, 2 * frows)), dma((2, 2 * frows)),
            dma((2, 2)), dma((2, 2)),
            dma((2, 2, depth)), dma((2, 2, depth)),
            dma((3, owners)), dma((3,)),
            dma((owners,)), dma((owners,)),
        ],
        compiler_params=pltpu.CompilerParams(
            collective_id=1, has_side_effects=True, vmem_limit_bytes=56 * MIB
        ),
    )(send, look, here, pattern.reshape(-1), initial, child_update)


def mul(a, b):
    return jnp.dot(a, b, preferred_element_type=jnp.float32, precision=HIGHEST)


def mul_t(a, b):
    return lax.dot_general(
        a, b, (((1,), (1,)), ((), ())), preferred_element_type=jnp.float32, precision=HIGHEST
    )


def factor_block(block, beside=None):
    n = block.shape[0]
    width = 16
    row_id = lax.broadcasted_iota(jnp.int32, (n, n), 0)
    lane_id = lax.broadcasted_iota(jnp.int32, (n, n), 1)
    eye = row_id == lane_id

    def body(step, carry):
        left, right = carry
        if beside is not None:
            beside(step)
        live = row_id < n - width * step
        for i in range(0, width, 2):
            c0 = jnp.broadcast_to(left[:, i:i + 1], (n, n))
            c1 = jnp.broadcast_to(left[:, i + 1:i + 2], (n, n))
            a, b, c = c0[i:i + 1], c0[i + 1:i + 2], c1[i + 1:i + 2]
            ratio = b / a
            inv = 1.0 / (c - b * ratio)
            below = (row_id > i + 1) & live
            g1 = (c1 - c0 * ratio) * inv
            g0 = jnp.where(below, c0 / a - g1 * ratio, jnp.where(row_id == i + 1, ratio, 0.0))
            g1 = jnp.where(below, g1, 0.0)
            left, right = (
                left - g0 * left[i:i + 1] - g1 * left[i + 1:i + 2],
                right - g0 * right[i:i + 1] - g1 * right[i + 1:i + 2],
            )
        left = pltpu.roll(jnp.concatenate([left[width:], left[:width]], axis=0), n - width, 1)
        right = jnp.concatenate([right[width:], right[:width]], axis=0)
        return left, right

    upper, inverse = lax.fori_loop(0, n // width, body, (block, eye.astype(jnp.float32)))
    scale = lax.rsqrt(jnp.sum(jnp.where(eye, upper, 0.0), axis=1, keepdims=True))
    return jnp.where(row_id <= lane_id, upper * scale, 0.0).T, inverse * scale


def factor_tile(tile_value, factor_ref, inverse_ref, beside=(None, None)):
    n = tile_value.shape[0]
    h = n // 2
    sym = 0.5 * (tile_value + tile_value.T)
    l0, t0 = factor_block(sym[:h, :h], beside[0])
    l10 = mul_t(sym[h:, :h], t0)
    l1, t1 = factor_block(sym[h:, h:] - mul_t(l10, l10), beside[1])
    zero = jnp.zeros((h, h), jnp.float32)
    factor_ref[:h, :h] = l0
    factor_ref[:h, h:] = zero
    factor_ref[h:, :h] = l10
    factor_ref[h:, h:] = l1
    inverse_ref[:h, :h] = t0
    inverse_ref[:h, h:] = zero
    inverse_ref[h:, :h] = -mul(t1, mul(l10, t0))
    inverse_ref[h:, h:] = t1


def split(x):
    high = x.astype(jnp.bfloat16)
    return high, (x - high.astype(jnp.float32)).astype(jnp.bfloat16)


def finish_kernel(front_ref, cols_ref, lead_ref, out_ref, f0_ref, i0_ref, f1_ref, i1_ref, own_ref):
    rows = lax.axis_size("row")
    frows, tile = front_ref.shape[0], front_ref.shape[1]
    me = lax.axis_index("sub") * rows + lax.axis_index("row")
    col = lax.axis_index("col")
    eye = (
        lax.broadcasted_iota(jnp.int32, (tile, tile), 0) == lax.broadcasted_iota(jnp.int32, (tile, tile), 1)
    ).astype(jnp.float32)

    factor_tile(lead_ref[0, 0], f0_ref, i0_ref)
    i0 = i0_ref[...]
    l10 = mul_t(lead_ref[1, 0], i0)
    factor_tile(lead_ref[1, 1] - mul_t(l10, l10), f1_ref, i1_ref)
    i1 = i1_ref[...]
    p0 = mul_t(lead_ref[2, 0], i0)
    own_ref[...] = p0
    p1 = mul_t(lead_ref[2, 1] - mul_t(p0, l10), i1)
    p0 = jnp.where(col == 0, eye, jnp.where(col == 1, 0.0, p0))
    p1 = jnp.where(col == 0, 0.0, jnp.where(col == 1, eye, p1))
    n1 = mul(p1, i1)
    n0 = mul(p0 - mul(n1, l10), i0)
    sign = jnp.where(col < 2, 1.0, -1.0)
    keep = jnp.where(col < 2, 0.0, 1.0)
    n0_high, n0_low = split(n0)
    n1_high, n1_low = split(n1)

    def dot_t(a, b):
        return lax.dot_general(a, b, (((1,), (1,)), ((), ())), preferred_element_type=jnp.float32)

    def body(m, carry):
        a0_high, a0_low = split(cols_ref[0, m])
        a1_high, a1_low = split(cols_ref[1, m])
        total = dot_t(a0_low, n0_high) + dot_t(a0_high, n0_low) + dot_t(a1_low, n1_high) + dot_t(a1_high, n1_low)
        total = total + dot_t(a0_high, n0_high) + dot_t(a1_high, n1_high)
        out_ref[m] = keep * front_ref[m] + sign * total
        return carry

    lax.fori_loop(0, frows, body, 0)

    @pl.when(me == 0)
    def _():
        out_ref[0] = jnp.where(col == 0, f0_ref[...], jnp.where(col == 1, 0.0, front_ref[0]))

    @pl.when((me == 1) & (col == 1))
    def _():
        out_ref[0] = f1_ref[...]

    @pl.when((me == 1) & (col > 1))
    def _():
        out_ref[0] = front_ref[0] - mul_t(mul_t(lead_ref[1, 0], i0_ref[...]), own_ref[...])


def finish(front, cols, lead):
    frows, tile, _ = front.shape
    vmem = pl.BlockSpec(memory_space=pltpu.VMEM)
    return pl.pallas_call(
        finish_kernel,
        out_shape=jax.ShapeDtypeStruct(front.shape, jnp.float32),
        in_specs=[vmem] * 3,
        out_specs=vmem,
        scratch_shapes=[pltpu.VMEM((tile, tile), jnp.float32)] * 5,
        compiler_params=pltpu.CompilerParams(vmem_limit_bytes=48 * MIB),
    )(front, cols, lead)


EXTRA = 2


def fast_tables(rmap, me, frows):
    owners = rmap.shape[2]
    maps = rmap.reshape(-1, owners)
    target = maps % owners
    index = jnp.arange(owners)
    before = index[None, None, :] < index[None, :, None]
    rank = jnp.sum(((target[:, None, :] == target[:, :, None]) & before).astype(jnp.int32), axis=2)
    over = rank > 0
    order = jnp.sum((over[:, None, :] & before).astype(jnp.int32), axis=2)
    flat_target, flat_over = target.reshape(-1), over.reshape(-1)
    flat = jnp.arange(owners * owners)
    seat = jnp.sum(
        (
            (flat_target[None, :] == flat_target[:, None]) & flat_over[None, :] & (flat[None, :] < flat[:, None])
        ).astype(jnp.int32),
        axis=1,
    ).reshape(owners, owners)
    fits = jnp.max(jnp.where(over, seat, 0)) < EXTRA

    own = (index == me)[:, None]
    mine = jnp.sum(jnp.where(own, target, 0), axis=0)
    mine_over = jnp.any(own & over, axis=0)
    mine_order = jnp.sum(jnp.where(own, order, 0), axis=0)
    mine_map = jnp.sum(jnp.where(own, maps, 0), axis=0)
    base_hit = (mine[None, :] == (index ^ me)[:, None]) & ~mine_over[None, :]
    base = jnp.sum(jnp.where(base_hit, index[None, :], 0), axis=1)
    over_hit = mine_over[None, :] & (mine_order[None, :] == jnp.arange(2)[:, None])
    over_index = jnp.sum(jnp.where(over_hit, index[None, :], 0), axis=1)
    near = (index ^ me)[:, None]
    spot = (near * 2 + order).reshape(-1)
    relay_hit = (
        flat_over[None, None, :]
        & (flat_target[None, None, :] == (index ^ me)[:, None, None])
        & (seat.reshape(-1)[None, None, :] == jnp.arange(EXTRA)[None, :, None])
    )
    relay = jnp.sum(jnp.where(relay_hit, spot[None, None, :], 0), axis=2).reshape(-1)
    place = jnp.where(over, owners + seat, near)
    wanted = jnp.arange(frows) * owners + me
    found = maps.reshape(2, -1)[None] == wanted[:, None, None]
    look = jnp.sum(jnp.where(found, place.reshape(2, -1)[None], 0), axis=2).reshape(-1)
    here = jnp.sum(found.astype(jnp.int32), axis=2).reshape(-1)
    lead_hit = mine_map[None, :] == jnp.arange(2)[:, None]
    lead_index = jnp.sum(jnp.where(lead_hit, index[None, :], 0), axis=1)
    lead_here = jnp.sum(lead_hit.astype(jnp.int32), axis=1)
    table = jnp.concatenate([base, over_index, relay, lead_index, lead_here, look, here]).astype(jnp.int32)
    return table, fits


def fast_kernel(
    table_ref, pattern_ref, initial_ref, child_ref, out_ref,
    out_buf, in_buf, over_src, over_mid, over_out, lead_part, lead_in, lead_strip, lead, cols, own_row,
    f0_ref, i0_ref, f1_ref, i1_ref, p0_ref,
    x_send, x_recv, o_send, o_recv, w_send, w_recv, l_send, l_recv, b_send, b_recv, g_send, g_recv,
    a_send, a_recv, c_send, c_recv, r_send, r_recv, h_send, h_recv,
):
    rows = lax.axis_size("row")
    owners = lax.axis_size("sub") * rows
    columns = lax.axis_size("col")
    depth = columns // 2
    frows, tile = initial_ref.shape[0], initial_ref.shape[2]
    half, strip = tile // 2, tile // owners
    sub, row, col = lax.axis_index("sub"), lax.axis_index("row"), lax.axis_index("col")
    me = sub * rows + row
    z, plane = col // 2, col % 2

    base_at, over_at = 0, owners
    relay_at = over_at + 2
    lead_at = relay_at + owners * EXTRA
    lead_here_at = lead_at + 2
    look_at = lead_here_at + 2
    here_at = look_at + 2 * frows

    def peer(delta):
        there = me ^ delta
        return (there // rows, there % rows, col)

    def line(delta):
        return (sub, row, col ^ delta)

    ways = ((sub, row, ((z + 1) % depth) * 2 + plane), (sub, row, ((z + depth - 1) % depth) * 2 + plane))

    def push(src, dst, send, recv, there):
        return pltpu.make_async_remote_copy(
            src_ref=src, dst_ref=dst, send_sem=send, recv_sem=recv, device_id=there, device_id_type=MESH
        )

    def strip_of(owner):
        return pl.ds(pl.multiple_of(owner * strip, strip), strip)

    def l_copy(delta):
        return push(
            lead_part.at[:, strip_of(me ^ delta)], lead_in.at[delta], l_send.at[delta], l_recv.at[delta], peer(delta)
        )

    def o_copy(delta):
        return push(
            over_src.at[:, strip_of(me ^ delta)], over_mid.at[pl.ds(2 * delta, 2)],
            o_send.at[delta], o_recv.at[delta], peer(delta),
        )

    def w_copy(delta, holder):
        return push(
            over_out.at[delta], in_buf.at[pl.ds(owners, EXTRA), strip_of(holder)],
            w_send.at[delta], w_recv.at[delta], peer(delta),
        )

    def x_copy(delta):
        return push(out_buf.at[delta], in_buf.at[delta], x_send.at[delta], x_recv.at[delta], peer(delta))

    def b_copy(delta, k):
        return push(lead_strip, lead.at[k, :, strip_of(me)], b_send.at[delta], b_recv.at[k], line(delta))

    def g_copy(delta, holder):
        part = lead.at[:, :, strip_of(holder)]
        return push(part, part, g_send.at[delta], g_recv.at[delta], peer(delta))

    barrier = pltpu.get_barrier_semaphore()
    for delta in range(1, owners):
        pl.semaphore_signal(barrier, inc=1, device_id=peer(delta), device_id_type=MESH)
    for delta in range(1, columns):
        pl.semaphore_signal(barrier, inc=1, device_id=line(delta), device_id_type=MESH)

    @pl.when(z == 0)
    def _():
        for p in range(2):
            value = jnp.where(table_ref[lead_here_at + p] > 0, child_ref[0, 0, table_ref[lead_at + p]], 0.0)
            first = initial_ref[0, 0] * pattern_ref[0].astype(jnp.float32)
            lead_part[p] = value + jnp.where(me == p, first, 0.0)

    for s in range(2):
        over_src[s] = child_ref[0, 0, table_ref[over_at + s]]

    def fill(delta, carry):
        out_buf[delta] = child_ref[0, 0, table_ref[base_at + delta]]
        return carry

    lax.fori_loop(1, owners, fill, 0)
    in_buf[0] = child_ref[0, 0, table_ref[base_at]]
    pl.semaphore_wait(barrier, owners - 1 + columns - 1)

    everyone = range(1, owners)
    first_part, second_part = 4, 8

    @pl.when(z == 0)
    def _():
        for delta in everyone:
            l_copy(delta).start()

    for delta in everyone:
        o_copy(delta).start()
    for delta in range(1, min(first_part, owners)):
        x_copy(delta).start()

    @pl.when(z == 0)
    def _():
        total = lead_part[:, strip_of(me)]
        for delta in everyone:
            l_copy(delta).wait_recv()
            total = total + lead_in[delta]
        lead_strip[...] = total
        lead[plane, :, strip_of(me)] = total
        for delta in range(1, columns):
            b_copy(delta, plane).start()

    for delta in everyone:
        o_copy(delta).wait_recv()
    for s in range(2):
        over_mid[s] = over_src[s, strip_of(me)]

    def relay(delta, carry):
        for e in range(EXTRA):
            over_out[delta, e] = over_mid[table_ref[relay_at + delta * EXTRA + e]]
        return carry

    lax.fori_loop(0, owners, relay, 0)
    for e in range(EXTRA):
        in_buf[owners + e, strip_of(me)] = over_out[0, e]
    for delta in everyone:
        w_copy(delta, me).start()
    for delta in range(first_part, min(second_part, owners)):
        x_copy(delta).start()
    for k in range(2):
        @pl.when(col != k)
        def _():
            b_copy(0, k).wait_recv()
    for delta in everyone:
        g_copy(delta, me).start()
    for delta in range(second_part, owners):
        x_copy(delta).start()
    for delta in everyone:
        g_copy(delta, me ^ delta).wait_recv()

    factor_tile(lead[0, 0], f0_ref, i0_ref)

    def tiles_arrive():
        for delta in everyone:
            x_copy(delta).wait_recv()
            w_copy(delta, me ^ delta).wait_recv()

    def assembled(m):
        value = initial_ref[m, 0] * pattern_ref[m].astype(jnp.float32)
        for c in range(2):
            tile_in = in_buf[table_ref[look_at + m * 2 + c]]
            value = value + jnp.where(table_ref[here_at + m * 2 + c] > 0, tile_in, 0.0)
        return value

    @pl.when(z == 0)
    def _():
        tiles_arrive()

        def body(m, carry):
            cols[plane, m] = assembled(m)
            return carry

        lax.fori_loop(0, frows, body, 0)

    quarter = half // 2
    units = 2 * frows
    hops = (z, (depth - z) % depth)

    def unit(k, h, i):
        return cols.at[k, i // 2, pl.ds(h * half + (i % 2) * quarter, quarter)]

    def a_copy(h, i):
        part = unit(plane, h, i)
        return push(part, part, a_send.at[h, i], a_recv.at[h, i], ways[h])

    def c_copy(k, h, i):
        part = unit(k, h, i)
        return push(part, part, c_send.at[h, i], c_recv.at[h, i], line(1))

    def a_step(step):
        for h in range(2):
            i = step - hops[h]
            live = (i >= 0) & (i < units)

            @pl.when(live & (z != 0))
            def _():
                a_copy(h, i).wait_recv()

            @pl.when(live & (hops[h] != depth - 1))
            def _():
                a_copy(h, i).start()

            @pl.when(live)
            def _():
                c_copy(plane, h, i).start()

    def a_steps(start, stop):
        def body(step, carry):
            a_step(step)
            return carry

        lax.fori_loop(start, stop, body, 0)

    i0 = i0_ref[...]
    l10 = mul_t(lead[0, 1], i0)
    factor_tile(lead[1, 1] - mul_t(l10, l10), f1_ref, i1_ref, (a_step, lambda step: a_step(step + 8)))

    steps = units + depth - 1
    done = 2 * (half // 16)
    for i in range(2):
        for h in range(2):
            c_copy(1 - plane, h, i).wait_recv()

    def r_copy(delta):
        there = strip_of(me ^ delta)
        return push(cols.at[:, 0, there], own_row.at[:, there], r_send.at[delta], r_recv.at[0], peer(delta))

    @pl.when(me == col)
    def _():
        for delta in everyone:
            r_copy(delta).start()
        own_row[:, strip_of(me)] = cols[:, 0, strip_of(me)]

    middle = done + (steps - done) // 2
    late = steps - 4
    a_steps(done, middle)

    @pl.when(me != col)
    def _():
        mine = strip_of(me)
        push(cols.at[:, 0, mine], own_row.at[:, mine], r_send.at[0], r_recv.at[0], line(1)).wait_recv()

    def h_copy(delta, holder):
        part = own_row.at[:, strip_of(holder)]
        return push(part, part, h_send.at[delta], h_recv.at[delta], peer(delta))

    for delta in everyone:
        h_copy(delta, me).start()
    a_steps(middle, late)
    for delta in everyone:
        h_copy(delta, me ^ delta).wait_recv()

    eye = (
        lax.broadcasted_iota(jnp.int32, (tile, tile), 0) == lax.broadcasted_iota(jnp.int32, (tile, tile), 1)
    ).astype(jnp.float32)
    i1 = i1_ref[...]
    p0 = mul_t(own_row[0], i0)
    p0_ref[...] = p0
    p1 = mul_t(own_row[1] - mul_t(p0, l10), i1)
    p0 = jnp.where(col == 0, eye, jnp.where(col == 1, 0.0, p0))
    p1 = jnp.where(col == 0, 0.0, jnp.where(col == 1, eye, p1))
    n1 = mul(p1, i1)
    n0 = mul(p0 - mul(n1, l10), i0)
    sign = jnp.where(col < 2, 1.0, -1.0)
    keep = jnp.where(col < 2, 0.0, 1.0)
    n0_high, n0_low = split(n0)
    n1_high, n1_low = split(n1)
    a_steps(late, steps)

    @pl.when(z != 0)
    def _():
        tiles_arrive()

    def crossed(i, carry):
        for h in range(2):
            c_copy(1 - plane, h, i).wait_recv()
        return carry

    lax.fori_loop(2, units, crossed, 0)

    def dot_t(a, b):
        return lax.dot_general(a, b, (((1,), (1,)), ((), ())), preferred_element_type=jnp.float32)

    def body(m, carry):
        a0_high, a0_low = split(cols[0, m])
        a1_high, a1_low = split(cols[1, m])
        total = dot_t(a0_low, n0_high) + dot_t(a0_high, n0_low) + dot_t(a1_low, n1_high) + dot_t(a1_high, n1_low)
        total = total + dot_t(a0_high, n0_high) + dot_t(a1_high, n1_high)
        out_ref[m] = keep * assembled(m) + sign * total
        return carry

    lax.fori_loop(0, frows, body, 0)

    @pl.when(me == 0)
    def _():
        out_ref[0] = jnp.where(col == 0, f0_ref[...], jnp.where(col == 1, 0.0, assembled(0)))

    @pl.when((me == 1) & (col == 1))
    def _():
        out_ref[0] = f1_ref[...]

    @pl.when((me == 1) & (col > 1))
    def _():
        out_ref[0] = assembled(0) - mul_t(l10, p0_ref[...])

    @pl.when(z == 0)
    def _():
        for delta in everyone:
            l_copy(delta).wait_send()
        for delta in range(1, columns):
            b_copy(delta, plane).wait_send()

    for delta in everyone:
        o_copy(delta).wait_send()
        w_copy(delta, me).wait_send()
        x_copy(delta).wait_send()
        g_copy(delta, me).wait_send()
        h_copy(delta, me).wait_send()

    @pl.when(me == col)
    def _():
        for delta in everyone:
            r_copy(delta).wait_send()

    def sent(i, carry):
        for h in range(2):
            @pl.when(hops[h] != depth - 1)
            def _():
                a_copy(h, i).wait_send()

            c_copy(plane, h, i).wait_send()
        return carry

    lax.fori_loop(0, units, sent, 0)


def fast(table, pattern, initial, child_update):
    owners = lax.axis_size("sub") * lax.axis_size("row")
    columns = lax.axis_size("col")
    frows, _, tile, _ = initial.shape
    strip, units = tile // owners, 2 * frows
    smem = pl.BlockSpec(memory_space=pltpu.SMEM)
    vmem = pl.BlockSpec(memory_space=pltpu.VMEM)
    dma = pltpu.SemaphoreType.DMA

    def room(*shape):
        return pltpu.VMEM(shape, jnp.float32)

    return pl.pallas_call(
        fast_kernel,
        out_shape=jax.ShapeDtypeStruct((frows, tile, tile), jnp.float32),
        in_specs=[smem] * 2 + [vmem] * 2,
        out_specs=vmem,
        scratch_shapes=[
            room(owners, tile, tile), room(owners + EXTRA, tile, tile),
            room(2, tile, tile), room(2 * owners, strip, tile), room(owners, EXTRA, strip, tile),
            room(2, tile, tile), room(owners, 2, strip, tile), room(2, strip, tile), room(2, 2, tile, tile),
            room(2, frows, tile, tile), room(2, tile, tile),
        ] + [room(tile, tile)] * 5 + [
            dma((owners,)), dma((owners,)), dma((owners,)), dma((owners,)), dma((owners,)), dma((owners,)),
            dma((owners,)), dma((owners,)), dma((columns,)), dma((2,)), dma((owners,)), dma((owners,)),
            dma((2, units)), dma((2, units)), dma((2, units)), dma((2, units)),
            dma((owners,)), dma((1,)), dma((owners,)), dma((owners,)),
        ],
        compiler_params=pltpu.CompilerParams(
            collective_id=0, has_side_effects=True, vmem_limit_bytes=56 * MIB
        ),
    )(table, pattern.reshape(-1), initial, child_update)


def general(table, pattern, initial, child_update, rmap):
    return finish(*exchange(initial, pattern, rmap, child_update))


def per_device(initial, pattern, rmap, child_update):
    me = lax.axis_index(("sub", "row"))
    table, fits = fast_tables(rmap, me, initial.shape[0])
    out = lax.cond(
        fits,
        lambda table, pattern, initial, child_update, rmap: fast(table, pattern, initial, child_update),
        general,
        table, pattern, initial, child_update, rmap,
    )
    return out[:, None]


def solution(mesh):
    return jax.shard_map(
        per_device,
        mesh=mesh,
        in_specs=(
            P(None, ("sub", "row"), None, "col"),
            P(None, ("sub", "row"), "col"),
            P(),
            P("sub", "row", None, None, "col"),
        ),
        out_specs=P(None, ("sub", "row"), None, "col"),
        check_vma=False,
    )
```

```python
import functools

import jax
import jax.numpy as jnp
from jax import lax
from jax.experimental import pallas as pl
from jax.experimental.pallas import tpu as pltpu
from jax.sharding import PartitionSpec as P

MESH = pl.DeviceIdType.MESH
MIB = 1024 * 1024
HIGHEST = lax.Precision.HIGHEST


def tables(rmap, owner_me, frows):
    owners = rmap.shape[2]
    maps = rmap.reshape(-1, owners)
    target = maps % owners
    index = jnp.arange(owners)
    earlier = (target[:, None, :] == target[:, :, None]) & (index[None, None, :] < index[None, :, None])
    rank = jnp.sum(earlier.astype(jnp.int32), axis=2)
    mine = jnp.sum(jnp.where((index == owner_me)[:, None], target, 0), axis=0)
    mine_rank = jnp.sum(jnp.where((index == owner_me)[:, None], rank, 0), axis=0)
    dest = index ^ owner_me
    hit = (mine[None, None, :] == dest[:, None, None]) & (mine_rank[None, None, :] == jnp.arange(2)[None, :, None])
    send = jnp.sum(jnp.where(hit, index[None, None, :], 0), axis=2).reshape(-1)
    place = (index ^ owner_me)[:, None] * 2 + rank
    wanted = jnp.arange(frows) * owners + owner_me
    found = maps.reshape(2, -1)[None] == wanted[:, None, None]
    look = jnp.sum(jnp.where(found, place.reshape(2, -1)[None], 0), axis=2)
    here = jnp.sum(found.astype(jnp.int32), axis=2)
    return send.astype(jnp.int32), look.reshape(-1).astype(jnp.int32), here.reshape(-1).astype(jnp.int32)


def exchange_kernel(
    send_ref, look_ref, here_ref, pattern_ref, initial_ref, child_ref,
    front_ref, cols_ref, lead_ref,
    out_buf, in_buf,
    x_send, x_recv, a_send, a_recv, c_send, c_recv, b_send, b_recv, s_send, s_recv, g_send, g_recv,
):
    rows = lax.axis_size("row")
    owners = lax.axis_size("sub") * rows
    depth = lax.axis_size("col") // 2
    frows, tile = initial_ref.shape[0], initial_ref.shape[2]
    half = tile // 2
    sub, row, col = lax.axis_index("sub"), lax.axis_index("row"), lax.axis_index("col")
    me = sub * rows + row
    z, plane = col // 2, col % 2
    other = 1 - plane

    def peer(delta):
        there = me ^ delta
        return (there // rows, there % rows, col)

    up = (sub, row, ((z + 1) % depth) * 2 + plane)
    down = (sub, row, ((z + depth - 1) % depth) * 2 + plane)
    across = (sub, row, z * 2 + other)
    ways = (up, down)

    barrier = pltpu.get_barrier_semaphore()
    for delta in range(1, owners):
        pl.semaphore_signal(barrier, inc=1, device_id=peer(delta), device_id_type=MESH)
    for there in (up, down, across):
        pl.semaphore_signal(barrier, inc=1, device_id=there, device_id_type=MESH)

    for s in range(2):
        out_buf[s] = child_ref[0, 0, send_ref[s]]

    def fill(delta, carry):
        for s in range(2):
            out_buf[delta * 2 + s] = child_ref[0, 0, send_ref[delta * 2 + s]]
        return carry

    lax.fori_loop(1, owners, fill, 0)
    for s in range(2):
        in_buf[s] = out_buf[s]
    pl.semaphore_wait(barrier, owners - 1 + 3)

    def x_copy(delta):
        part = pl.ds(delta * 2, 2)
        return pltpu.make_async_remote_copy(
            src_ref=out_buf.at[part], dst_ref=in_buf.at[part], send_sem=x_send.at[delta],
            recv_sem=x_recv.at[delta], device_id=peer(delta), device_id_type=MESH,
        )

    for delta in range(1, owners):
        x_copy(delta).start()
    for delta in range(1, owners):
        x_copy(delta).wait_recv()

    def assemble(m, carry):
        value = initial_ref[m, 0] * pattern_ref[m].astype(jnp.float32)
        for c in range(2):
            tile_in = in_buf[look_ref[m * 2 + c]]
            value = value + jnp.where(here_ref[m * 2 + c] > 0, tile_in, 0.0)
        front_ref[m] = value

        @pl.when(z == 0)
        def _():
            cols_ref[plane, m] = value

        return carry

    lax.fori_loop(0, frows, assemble, 0)

    quarter = half // 2

    def a_copy(h, i):
        part = cols_ref.at[plane, i // 2, pl.ds(h * half + (i % 2) * quarter, quarter)]
        return pltpu.make_async_remote_copy(
            src_ref=part, dst_ref=part, send_sem=a_send.at[h, i], recv_sem=a_recv.at[h, i],
            device_id=ways[h], device_id_type=MESH,
        )

    hops = (z, (depth - z) % depth)

    def a_step(step, carry):
        for h in range(2):
            i = step - hops[h]
            live = (i >= 0) & (i < 2 * frows)

            @pl.when(live & (z != 0))
            def _():
                a_copy(h, i).wait_recv()

            @pl.when(live & (hops[h] != depth - 1))
            def _():
                a_copy(h, i).start()

        return carry

    lax.fori_loop(0, 2 * frows + depth - 1, a_step, 0)

    piece = half // depth
    group = frows // 2

    def cut(k, h, g, origin):
        return cols_ref.at[k, pl.ds(g * group, group), pl.ds(h * half + origin * piece, piece)]

    def c_copy(k, h, g):
        part = cut(k, h, g, z)
        return pltpu.make_async_remote_copy(
            src_ref=part, dst_ref=part, send_sem=c_send.at[h, g], recv_sem=c_recv.at[h, g],
            device_id=across, device_id_type=MESH,
        )

    for g in range(2):
        for h in range(2):
            c_copy(plane, h, g).start()

    def b_copy(h, g, t, origin):
        part = cut(other, h, g, origin)
        return pltpu.make_async_remote_copy(
            src_ref=part, dst_ref=part, send_sem=b_send.at[h, g, t], recv_sem=b_recv.at[h, g, t],
            device_id=ways[h], device_id_type=MESH,
        )

    def origin_of(h, t):
        return (z + depth - t) % depth if h == 0 else (z + t) % depth

    for g in range(2):
        for h in range(2):
            c_copy(other, h, g).wait_recv()
            b_copy(h, g, 0, origin_of(h, 0)).start()

    def b_step(t, carry):
        for g in range(2):
            for h in range(2):
                b_copy(h, g, t - 1, origin_of(h, t)).wait_recv()

                @pl.when(t < depth - 1)
                def _():
                    b_copy(h, g, t, origin_of(h, t)).start()

        return carry

    lax.fori_loop(1, depth, b_step, 0)

    strip = tile // owners
    sources = (0, 1, col % owners)

    def s_copy(s, delta):
        rows_there = pl.ds((me ^ delta) * strip, strip)
        return pltpu.make_async_remote_copy(
            src_ref=cols_ref.at[:, 0, rows_there], dst_ref=lead_ref.at[s, :, rows_there],
            send_sem=s_send.at[s, delta], recv_sem=s_recv.at[s], device_id=peer(delta), device_id_type=MESH,
        )

    for s, source in enumerate(sources):
        @pl.when(me == source)
        def _():
            for delta in range(1, owners):
                s_copy(s, delta).start()
            mine = pl.ds(pl.multiple_of(me * strip, strip), strip)
            lead_ref[s, :, mine] = cols_ref[:, 0, mine]

    def s_arrival(s):
        mine = pl.ds(me * strip, strip)
        return pltpu.make_async_remote_copy(
            src_ref=cols_ref.at[:, 0, mine], dst_ref=lead_ref.at[s, :, mine],
            send_sem=s_send.at[s, 0], recv_sem=s_recv.at[s], device_id=across, device_id_type=MESH,
        )

    for s, source in enumerate(sources):
        @pl.when(me != source)
        def _():
            s_arrival(s).wait_recv()

    def g_copy(delta, holder):
        part = lead_ref.at[:, :, pl.ds(holder * strip, strip)]
        return pltpu.make_async_remote_copy(
            src_ref=part, dst_ref=part, send_sem=g_send.at[delta], recv_sem=g_recv.at[delta],
            device_id=peer(delta), device_id_type=MESH,
        )

    for delta in range(1, owners):
        g_copy(delta, me).start()
    for delta in range(1, owners):
        g_copy(delta, me ^ delta).wait_recv()

    for delta in range(1, owners):
        g_copy(delta, me).wait_send()
        x_copy(delta).wait_send()
    for s, source in enumerate(sources):
        @pl.when(me == source)
        def _():
            for delta in range(1, owners):
                s_copy(s, delta).wait_send()
    for g in range(2):
        for h in range(2):
            c_copy(plane, h, g).wait_send()

    def b_end(t, carry):
        for g in range(2):
            for h in range(2):
                b_copy(h, g, t, origin_of(h, t)).wait_send()
        return carry

    lax.fori_loop(0, depth - 1, b_end, 0)

    def a_end(i, carry):
        for h in range(2):
            @pl.when(hops[h] != depth - 1)
            def _():
                a_copy(h, i).wait_send()
        return carry

    lax.fori_loop(0, 2 * frows, a_end, 0)


def exchange(initial, pattern, rmap, child_update):
    owners = lax.axis_size("sub") * lax.axis_size("row")
    depth = lax.axis_size("col") // 2
    frows, _, tile, _ = initial.shape
    me = lax.axis_index(("sub", "row"))
    send, look, here = tables(rmap, me, frows)
    smem = pl.BlockSpec(memory_space=pltpu.SMEM)
    vmem = pl.BlockSpec(memory_space=pltpu.VMEM)
    dma = pltpu.SemaphoreType.DMA
    return pl.pallas_call(
        exchange_kernel,
        out_shape=(
            jax.ShapeDtypeStruct((frows, tile, tile), jnp.float32),
            jax.ShapeDtypeStruct((2, frows, tile, tile), jnp.float32),
            jax.ShapeDtypeStruct((3, 2, tile, tile), jnp.float32),
        ),
        in_specs=[smem] * 4 + [vmem] * 2,
        out_specs=(vmem, vmem, vmem),
        scratch_shapes=[
            pltpu.VMEM((2 * owners, tile, tile), jnp.float32),
            pltpu.VMEM((2 * owners, tile, tile), jnp.float32),
            dma((owners,)), dma((owners,)),
            dma((2, 2 * frows)), dma((2, 2 * frows)),
            dma((2, 2)), dma((2, 2)),
            dma((2, 2, depth)), dma((2, 2, depth)),
            dma((3, owners)), dma((3,)),
            dma((owners,)), dma((owners,)),
        ],
        compiler_params=pltpu.CompilerParams(
            collective_id=1, has_side_effects=True, vmem_limit_bytes=56 * MIB
        ),
    )(send, look, here, pattern.reshape(-1), initial, child_update)


def mul(a, b):
    return jnp.dot(a, b, preferred_element_type=jnp.float32, precision=HIGHEST)


def mul_t(a, b):
    return lax.dot_general(
        a, b, (((1,), (1,)), ((), ())), preferred_element_type=jnp.float32, precision=HIGHEST
    )


def factor_block(block, beside=None):
    n = block.shape[0]
    width = 16
    row_id = lax.broadcasted_iota(jnp.int32, (n, n), 0)
    lane_id = lax.broadcasted_iota(jnp.int32, (n, n), 1)
    eye = row_id == lane_id

    def body(step, carry):
        left, right = carry
        if beside is not None:
            beside(step)
        live = row_id < n - width * step
        for i in range(0, width, 2):
            c0 = jnp.broadcast_to(left[:, i:i + 1], (n, n))
            c1 = jnp.broadcast_to(left[:, i + 1:i + 2], (n, n))
            a, b, c = c0[i:i + 1], c0[i + 1:i + 2], c1[i + 1:i + 2]
            ratio = b / a
            inv = 1.0 / (c - b * ratio)
            below = (row_id > i + 1) & live
            g1 = (c1 - c0 * ratio) * inv
            g0 = jnp.where(below, c0 / a - g1 * ratio, jnp.where(row_id == i + 1, ratio, 0.0))
            g1 = jnp.where(below, g1, 0.0)
            left, right = (
                left - g0 * left[i:i + 1] - g1 * left[i + 1:i + 2],
                right - g0 * right[i:i + 1] - g1 * right[i + 1:i + 2],
            )
        left = pltpu.roll(jnp.concatenate([left[width:], left[:width]], axis=0), n - width, 1)
        right = jnp.concatenate([right[width:], right[:width]], axis=0)
        return left, right

    upper, inverse = lax.fori_loop(0, n // width, body, (block, eye.astype(jnp.float32)))
    scale = lax.rsqrt(jnp.sum(jnp.where(eye, upper, 0.0), axis=1, keepdims=True))
    return jnp.where(row_id <= lane_id, upper * scale, 0.0).T, inverse * scale


def factor_tile(tile_value, factor_ref, inverse_ref, beside=(None, None)):
    n = tile_value.shape[0]
    h = n // 2
    sym = 0.5 * (tile_value + tile_value.T)
    l0, t0 = factor_block(sym[:h, :h], beside[0])
    l10 = mul_t(sym[h:, :h], t0)
    l1, t1 = factor_block(sym[h:, h:] - mul_t(l10, l10), beside[1])
    zero = jnp.zeros((h, h), jnp.float32)
    factor_ref[:h, :h] = l0
    factor_ref[:h, h:] = zero
    factor_ref[h:, :h] = l10
    factor_ref[h:, h:] = l1
    inverse_ref[:h, :h] = t0
    inverse_ref[:h, h:] = zero
    inverse_ref[h:, :h] = -mul(t1, mul(l10, t0))
    inverse_ref[h:, h:] = t1


def split(x):
    high = x.astype(jnp.bfloat16)
    return high, (x - high.astype(jnp.float32)).astype(jnp.bfloat16)


def finish_kernel(front_ref, cols_ref, lead_ref, out_ref, f0_ref, i0_ref, f1_ref, i1_ref, own_ref):
    rows = lax.axis_size("row")
    frows, tile = front_ref.shape[0], front_ref.shape[1]
    me = lax.axis_index("sub") * rows + lax.axis_index("row")
    col = lax.axis_index("col")
    eye = (
        lax.broadcasted_iota(jnp.int32, (tile, tile), 0) == lax.broadcasted_iota(jnp.int32, (tile, tile), 1)
    ).astype(jnp.float32)

    factor_tile(lead_ref[0, 0], f0_ref, i0_ref)
    i0 = i0_ref[...]
    l10 = mul_t(lead_ref[1, 0], i0)
    factor_tile(lead_ref[1, 1] - mul_t(l10, l10), f1_ref, i1_ref)
    i1 = i1_ref[...]
    p0 = mul_t(lead_ref[2, 0], i0)
    own_ref[...] = p0
    p1 = mul_t(lead_ref[2, 1] - mul_t(p0, l10), i1)
    p0 = jnp.where(col == 0, eye, jnp.where(col == 1, 0.0, p0))
    p1 = jnp.where(col == 0, 0.0, jnp.where(col == 1, eye, p1))
    n1 = mul(p1, i1)
    n0 = mul(p0 - mul(n1, l10), i0)
    sign = jnp.where(col < 2, 1.0, -1.0)
    keep = jnp.where(col < 2, 0.0, 1.0)
    n0_high, n0_low = split(n0)
    n1_high, n1_low = split(n1)

    def dot_t(a, b):
        return lax.dot_general(a, b, (((1,), (1,)), ((), ())), preferred_element_type=jnp.float32)

    def body(m, carry):
        a0_high, a0_low = split(cols_ref[0, m])
        a1_high, a1_low = split(cols_ref[1, m])
        total = dot_t(a0_low, n0_high) + dot_t(a0_high, n0_low) + dot_t(a1_low, n1_high) + dot_t(a1_high, n1_low)
        total = total + dot_t(a0_high, n0_high) + dot_t(a1_high, n1_high)
        out_ref[m] = keep * front_ref[m] + sign * total
        return carry

    lax.fori_loop(0, frows, body, 0)

    @pl.when(me == 0)
    def _():
        out_ref[0] = jnp.where(col == 0, f0_ref[...], jnp.where(col == 1, 0.0, front_ref[0]))

    @pl.when((me == 1) & (col == 1))
    def _():
        out_ref[0] = f1_ref[...]

    @pl.when((me == 1) & (col > 1))
    def _():
        out_ref[0] = front_ref[0] - mul_t(mul_t(lead_ref[1, 0], i0_ref[...]), own_ref[...])


def finish(front, cols, lead):
    frows, tile, _ = front.shape
    vmem = pl.BlockSpec(memory_space=pltpu.VMEM)
    return pl.pallas_call(
        finish_kernel,
        out_shape=jax.ShapeDtypeStruct(front.shape, jnp.float32),
        in_specs=[vmem] * 3,
        out_specs=vmem,
        scratch_shapes=[pltpu.VMEM((tile, tile), jnp.float32)] * 5,
        compiler_params=pltpu.CompilerParams(vmem_limit_bytes=48 * MIB),
    )(front, cols, lead)


EXTRA = 2
SLABS = 4


def fast_tables(rmap, me, frows):
    owners = rmap.shape[2]
    maps = rmap.reshape(-1, owners)
    target = maps % owners
    index = jnp.arange(owners)
    before = index[None, None, :] < index[None, :, None]
    rank = jnp.sum(((target[:, None, :] == target[:, :, None]) & before).astype(jnp.int32), axis=2)
    over = rank > 0
    order = jnp.sum((over[:, None, :] & before).astype(jnp.int32), axis=2)
    flat_target, flat_over = target.reshape(-1), over.reshape(-1)
    flat = jnp.arange(owners * owners)
    seat = jnp.sum(
        (
            (flat_target[None, :] == flat_target[:, None]) & flat_over[None, :] & (flat[None, :] < flat[:, None])
        ).astype(jnp.int32),
        axis=1,
    ).reshape(owners, owners)
    fits = jnp.max(jnp.where(over, seat, 0)) < EXTRA

    own = (index == me)[:, None]
    mine = jnp.sum(jnp.where(own, target, 0), axis=0)
    mine_over = jnp.any(own & over, axis=0)
    mine_order = jnp.sum(jnp.where(own, order, 0), axis=0)
    mine_map = jnp.sum(jnp.where(own, maps, 0), axis=0)
    base_hit = (mine[None, :] == (index ^ me)[:, None]) & ~mine_over[None, :]
    base = jnp.sum(jnp.where(base_hit, index[None, :], 0), axis=1)
    over_hit = mine_over[None, :] & (mine_order[None, :] == jnp.arange(2)[:, None])
    over_index = jnp.sum(jnp.where(over_hit, index[None, :], 0), axis=1)
    near = (index ^ me)[:, None]
    spot = (near * 2 + order).reshape(-1)
    relay_hit = (
        flat_over[None, None, :]
        & (flat_target[None, None, :] == (index ^ me)[:, None, None])
        & (seat.reshape(-1)[None, None, :] == jnp.arange(EXTRA)[None, :, None])
    )
    relay = jnp.sum(jnp.where(relay_hit, spot[None, None, :], 0), axis=2).reshape(-1)
    place = jnp.where(over, owners + seat, near)
    wanted = jnp.arange(frows) * owners + me
    found = maps.reshape(2, -1)[None] == wanted[:, None, None]
    look = jnp.sum(jnp.where(found, place.reshape(2, -1)[None], 0), axis=2).reshape(-1)
    here = jnp.sum(found.astype(jnp.int32), axis=2).reshape(-1)
    lead_hit = mine_map[None, :] == jnp.arange(2)[:, None]
    lead_index = jnp.sum(jnp.where(lead_hit, index[None, :], 0), axis=1)
    lead_here = jnp.sum(lead_hit.astype(jnp.int32), axis=1)
    table = jnp.concatenate([base, over_index, relay, lead_index, lead_here, look, here]).astype(jnp.int32)
    return table, fits


def fast_kernel(
    table_ref, pattern_ref, initial_ref, child_ref, out_ref,
    out_buf, in_0, in_1, in_2, in_3, over_in, over_src, over_mid, over_out, lead_part, lead_in, lead_strip, lead, cols, own_row,
    f0_ref, i0_ref, f1_ref, i1_ref, p0_ref,
    x_send, x_recv, o_send, o_recv, w_send, w_recv, l_send, l_recv, b_send, b_recv, g_send, g_recv,
    a_send, a_recv, c_send, c_recv, r_send, r_recv, h_send, h_recv,
):
    rows = lax.axis_size("row")
    owners = lax.axis_size("sub") * rows
    columns = lax.axis_size("col")
    depth = columns // 2
    frows, tile = initial_ref.shape[0], initial_ref.shape[2]
    half, strip, slab = tile // 2, tile // owners, tile // SLABS
    in_slabs = (in_0, in_1, in_2, in_3)
    sub, row, col = lax.axis_index("sub"), lax.axis_index("row"), lax.axis_index("col")
    me = sub * rows + row
    z, plane = col // 2, col % 2

    base_at, over_at = 0, owners
    relay_at = over_at + 2
    lead_at = relay_at + owners * EXTRA
    lead_here_at = lead_at + 2
    look_at = lead_here_at + 2
    here_at = look_at + 2 * frows

    def peer(delta):
        there = me ^ delta
        return (there // rows, there % rows, col)

    def line(delta):
        return (sub, row, col ^ delta)

    ways = ((sub, row, ((z + 1) % depth) * 2 + plane), (sub, row, ((z + depth - 1) % depth) * 2 + plane))

    def push(src, dst, send, recv, there):
        return pltpu.make_async_remote_copy(
            src_ref=src, dst_ref=dst, send_sem=send, recv_sem=recv, device_id=there, device_id_type=MESH
        )

    def strip_of(owner):
        return pl.ds(pl.multiple_of(owner * strip, strip), strip)

    def l_copy(delta):
        return push(
            lead_part.at[:, strip_of(me ^ delta)], lead_in.at[delta], l_send.at[delta], l_recv.at[delta], peer(delta)
        )

    def o_copy(delta):
        return push(
            over_src.at[:, strip_of(me ^ delta)], over_mid.at[pl.ds(2 * delta, 2)],
            o_send.at[delta], o_recv.at[delta], peer(delta),
        )

    def w_copy(delta, holder):
        return push(
            over_out.at[delta], over_in.at[:, strip_of(holder)],
            w_send.at[delta], w_recv.at[delta], peer(delta),
        )

    def x_copy(delta, c):
        part = pl.ds(c * slab, slab)
        return push(
            out_buf.at[delta, part], in_slabs[c].at[delta], x_send.at[c, delta], x_recv.at[c, delta], peer(delta)
        )

    def b_copy(delta, k):
        return push(lead_strip, lead.at[k, :, strip_of(me)], b_send.at[delta], b_recv.at[k], line(delta))

    def g_copy(delta, holder):
        part = lead.at[:, :, strip_of(holder)]
        return push(part, part, g_send.at[delta], g_recv.at[delta], peer(delta))

    barrier = pltpu.get_barrier_semaphore()
    for delta in range(1, owners):
        pl.semaphore_signal(barrier, inc=1, device_id=peer(delta), device_id_type=MESH)
    for delta in range(1, columns):
        pl.semaphore_signal(barrier, inc=1, device_id=line(delta), device_id_type=MESH)

    @pl.when(z == 0)
    def _():
        for p in range(2):
            value = jnp.where(table_ref[lead_here_at + p] > 0, child_ref[0, 0, table_ref[lead_at + p]], 0.0)
            first = initial_ref[0, 0] * pattern_ref[0].astype(jnp.float32)
            lead_part[p] = value + jnp.where(me == p, first, 0.0)

    for s in range(2):
        over_src[s] = child_ref[0, 0, table_ref[over_at + s]]

    def fill(delta, carry):
        out_buf[delta] = child_ref[0, 0, table_ref[base_at + delta]]
        return carry

    lax.fori_loop(1, owners, fill, 0)
    for c in range(SLABS):
        in_slabs[c][0] = child_ref[0, 0, table_ref[base_at], pl.ds(c * slab, slab)]
    pl.semaphore_wait(barrier, owners - 1 + columns - 1)

    everyone = range(1, owners)
    @pl.when(z == 0)
    def _():
        for delta in everyone:
            l_copy(delta).start()

    for delta in everyone:
        o_copy(delta).start()
    for delta in everyone:
        x_copy(delta, 0).start()

    @pl.when(z == 0)
    def _():
        total = lead_part[:, strip_of(me)]
        for delta in everyone:
            l_copy(delta).wait_recv()
            total = total + lead_in[delta]
        lead_strip[...] = total
        lead[plane, :, strip_of(me)] = total
        for delta in range(1, columns):
            b_copy(delta, plane).start()

    for delta in everyone:
        o_copy(delta).wait_recv()
    for s in range(2):
        over_mid[s] = over_src[s, strip_of(me)]

    def relay(delta, carry):
        for e in range(EXTRA):
            over_out[delta, e] = over_mid[table_ref[relay_at + delta * EXTRA + e]]
        return carry

    lax.fori_loop(0, owners, relay, 0)
    for e in range(EXTRA):
        over_in[e, strip_of(me)] = over_out[0, e]
    for delta in everyone:
        w_copy(delta, me).start()
    for delta in everyone:
        x_copy(delta, 1).start()
    for k in range(2):
        @pl.when(col != k)
        def _():
            b_copy(0, k).wait_recv()
    for delta in everyone:
        g_copy(delta, me).start()
    for c in range(2, SLABS):
        for delta in everyone:
            x_copy(delta, c).start()

    def slab_arrives(c):
        for delta in everyone:
            x_copy(delta, c).wait_recv()
            if c == 0:
                w_copy(delta, me ^ delta).wait_recv()

    def assembled_slab(m, c):
        part = pl.ds(c * slab, slab)
        value = initial_ref[m, 0, part] * pattern_ref[m].astype(jnp.float32)
        for child in range(2):
            spot = table_ref[look_at + m * 2 + child]
            direct = in_slabs[c][jnp.minimum(spot, owners - 1)]
            relayed = over_in[jnp.maximum(spot - owners, 0), part]
            tile_in = jnp.where(spot < owners, direct, relayed)
            value = value + jnp.where(table_ref[here_at + m * 2 + child] > 0, tile_in, 0.0)
        return value

    def assembled(m):
        return jnp.concatenate([assembled_slab(m, c) for c in range(SLABS)], axis=0)

    def each(start, stop, do):
        def body(i, carry):
            do(i)
            return carry

        lax.fori_loop(start, stop, body, 0)

    def root_slab(c):
        slab_arrives(c)
        part = pl.ds(c * slab, slab)

        def fill_column(m):
            cols[plane, m, part] = assembled_slab(m, c)

        each(0, frows, fill_column)

    units = SLABS * frows
    turn = depth // 2
    feeds = (z < turn, (z == 0) | (z > turn + 1))

    def unit(k, i):
        third = i < 3 * frows + 1
        lead_unit = i < 2 * frows + 2
        c = jnp.where(i < 2 * frows, i // frows, jnp.where(lead_unit, i - 2 * frows + 2, jnp.where(third, 2, 3)))
        m = jnp.where(
            i < 2 * frows, i % frows,
            jnp.where(lead_unit, 0, jnp.where(third, i - 2 * frows - 1, i - 3 * frows)),
        )
        return cols.at[k, m, pl.ds(pl.multiple_of(c * slab, slab), slab)]

    def a_copy(h, i):
        part = unit(plane, i)
        return push(part, part, a_send.at[h, i], a_recv.at[i], ways[h])

    def c_copy(k, i):
        part = unit(k, i)
        return push(part, part, c_send.at[i], c_recv.at[i], line(1))

    def a_step(i):
        @pl.when(z != 0)
        def _():
            a_copy(0, i).wait_recv()

        for h in range(2):
            @pl.when(feeds[h])
            def _():
                a_copy(h, i).start()

        c_copy(plane, i).start()

    turns = half // 16
    ahead = units - 4 * turns

    def gate(c, ready):
        @pl.when(ready & (z == 0))
        def _():
            root_slab(c)

    def beside(block):
        def do(step):
            i = ahead + block * turns + step
            for c, first in ((2, 2 * frows), (3, 2 * frows + 1)):
                if ahead + block * turns <= first < ahead + (block + 1) * turns:
                    gate(c, i == first)
            a_step(i)

        return do

    gate(0, True)
    each(0, frows, a_step)
    gate(1, True)
    each(frows, ahead, a_step)
    for delta in everyone:
        g_copy(delta, me ^ delta).wait_recv()
    factor_tile(lead[0, 0], f0_ref, i0_ref, (beside(0), beside(1)))

    early = (0, frows, 2 * frows, 2 * frows + 1)
    for i in early:
        c_copy(1 - plane, i).wait_recv()

    def r_copy(delta):
        there = strip_of(me ^ delta)
        return push(cols.at[:, 0, there], own_row.at[:, there], r_send.at[delta], r_recv.at[0], peer(delta))

    @pl.when(me == col)
    def _():
        for delta in everyone:
            r_copy(delta).start()
        own_row[:, strip_of(me)] = cols[:, 0, strip_of(me)]

    i0 = i0_ref[...]
    l10 = mul_t(lead[0, 1], i0)

    def h_copy(delta, holder):
        part = own_row.at[:, strip_of(holder)]
        return push(part, part, h_send.at[delta], h_recv.at[delta], peer(delta))

    def spread_row(step):
        @pl.when(step == 0)
        def _():
            @pl.when(me != col)
            def _():
                mine = strip_of(me)
                push(
                    cols.at[:, 0, mine], own_row.at[:, mine], r_send.at[0], r_recv.at[0], line(1)
                ).wait_recv()

            for delta in everyone:
                h_copy(delta, me).start()

        beside(3)(step)

    factor_tile(lead[1, 1] - mul_t(l10, l10), f1_ref, i1_ref, (beside(2), spread_row))
    for delta in everyone:
        h_copy(delta, me ^ delta).wait_recv()

    eye = (
        lax.broadcasted_iota(jnp.int32, (tile, tile), 0) == lax.broadcasted_iota(jnp.int32, (tile, tile), 1)
    ).astype(jnp.float32)
    i1 = i1_ref[...]
    p0 = mul_t(own_row[0], i0)
    p0_ref[...] = p0
    p1 = mul_t(own_row[1] - mul_t(p0, l10), i1)
    p0 = jnp.where(col == 0, eye, jnp.where(col == 1, 0.0, p0))
    p1 = jnp.where(col == 0, 0.0, jnp.where(col == 1, eye, p1))
    n1 = mul(p1, i1)
    n0 = mul(p0 - mul(n1, l10), i0)
    sign = jnp.where(col < 2, 1.0, -1.0)
    keep = jnp.where(col < 2, 0.0, 1.0)
    n0_high, n0_low = split(n0)
    n1_high, n1_low = split(n1)

    @pl.when(z != 0)
    def _():
        for c in range(SLABS):
            slab_arrives(c)

    def dot_t(a, b):
        return lax.dot_general(a, b, (((1,), (1,)), ((), ())), preferred_element_type=jnp.float32)

    def update(m):
        a0_high, a0_low = split(cols[0, m])
        a1_high, a1_low = split(cols[1, m])
        total = dot_t(a0_low, n0_high) + dot_t(a0_high, n0_low) + dot_t(a1_low, n1_high) + dot_t(a1_high, n1_low)
        total = total + dot_t(a0_high, n0_high) + dot_t(a1_high, n1_high)
        out_ref[m] = keep * assembled(m) + sign * total

    def last(m):
        for start in (0, frows, 2 * frows + 1, 3 * frows):
            c_copy(1 - plane, start + m).wait_recv()
        update(m)

    update(0)
    each(1, frows, last)

    @pl.when(me == 0)
    def _():
        out_ref[0] = jnp.where(col == 0, f0_ref[...], jnp.where(col == 1, 0.0, assembled(0)))

    @pl.when((me == 1) & (col == 1))
    def _():
        out_ref[0] = f1_ref[...]

    @pl.when((me == 1) & (col > 1))
    def _():
        out_ref[0] = assembled(0) - mul_t(l10, p0_ref[...])

    @pl.when(z == 0)
    def _():
        for delta in everyone:
            l_copy(delta).wait_send()
        for delta in range(1, columns):
            b_copy(delta, plane).wait_send()

    for delta in everyone:
        o_copy(delta).wait_send()
        w_copy(delta, me).wait_send()
        for c in range(SLABS):
            x_copy(delta, c).wait_send()
        g_copy(delta, me).wait_send()
        h_copy(delta, me).wait_send()

    @pl.when(me == col)
    def _():
        for delta in everyone:
            r_copy(delta).wait_send()

    def sent(i):
        for h in range(2):
            @pl.when(feeds[h])
            def _():
                a_copy(h, i).wait_send()

        c_copy(plane, i).wait_send()

    each(0, units, sent)


def fast(table, pattern, initial, child_update):
    owners = lax.axis_size("sub") * lax.axis_size("row")
    columns = lax.axis_size("col")
    frows, _, tile, _ = initial.shape
    strip, units = tile // owners, SLABS * frows
    smem = pl.BlockSpec(memory_space=pltpu.SMEM)
    vmem = pl.BlockSpec(memory_space=pltpu.VMEM)
    dma = pltpu.SemaphoreType.DMA

    def room(*shape):
        return pltpu.VMEM(shape, jnp.float32)

    return pl.pallas_call(
        fast_kernel,
        out_shape=jax.ShapeDtypeStruct((frows, tile, tile), jnp.float32),
        in_specs=[smem] * 2 + [vmem] * 2,
        out_specs=vmem,
        scratch_shapes=[
            room(owners, tile, tile), *[room(owners, tile // SLABS, tile)] * SLABS, room(EXTRA, tile, tile),
            room(2, tile, tile), room(2 * owners, strip, tile), room(owners, EXTRA, strip, tile),
            room(2, tile, tile), room(owners, 2, strip, tile), room(2, strip, tile), room(2, 2, tile, tile),
            room(2, frows, tile, tile), room(2, tile, tile),
        ] + [room(tile, tile)] * 5 + [
            dma((SLABS, owners)), dma((SLABS, owners)), dma((owners,)), dma((owners,)), dma((owners,)), dma((owners,)),
            dma((owners,)), dma((owners,)), dma((columns,)), dma((2,)), dma((owners,)), dma((owners,)),
            dma((2, units)), dma((units,)), dma((units,)), dma((units,)),
            dma((owners,)), dma((1,)), dma((owners,)), dma((owners,)),
        ],
        compiler_params=pltpu.CompilerParams(
            collective_id=0, has_side_effects=True, vmem_limit_bytes=56 * MIB
        ),
    )(table, pattern.reshape(-1), initial, child_update)


def general(table, pattern, initial, child_update, rmap):
    return finish(*exchange(initial, pattern, rmap, child_update))


def per_device(initial, pattern, rmap, child_update):
    me = lax.axis_index(("sub", "row"))
    table, fits = fast_tables(rmap, me, initial.shape[0])
    out = lax.cond(
        fits,
        lambda table, pattern, initial, child_update, rmap: fast(table, pattern, initial, child_update),
        general,
        table, pattern, initial, child_update, rmap,
    )
    return out[:, None]


def solution(mesh):
    return jax.shard_map(
        per_device,
        mesh=mesh,
        in_specs=(
            P(None, ("sub", "row"), None, "col"),
            P(None, ("sub", "row"), "col"),
            P(),
            P("sub", "row", None, None, "col"),
        ),
        out_specs=P(None, ("sub", "row"), None, "col"),
        check_vma=False,
    )
```

```python
import functools

import jax
import jax.numpy as jnp
from jax import lax
from jax.experimental import pallas as pl
from jax.experimental.pallas import tpu as pltpu
from jax.sharding import PartitionSpec as P

MESH = pl.DeviceIdType.MESH
MIB = 1024 * 1024
HIGHEST = lax.Precision.HIGHEST


def tables(rmap, owner_me, frows):
    owners = rmap.shape[2]
    maps = rmap.reshape(-1, owners)
    target = maps % owners
    index = jnp.arange(owners)
    earlier = (target[:, None, :] == target[:, :, None]) & (index[None, None, :] < index[None, :, None])
    rank = jnp.sum(earlier.astype(jnp.int32), axis=2)
    mine = jnp.sum(jnp.where((index == owner_me)[:, None], target, 0), axis=0)
    mine_rank = jnp.sum(jnp.where((index == owner_me)[:, None], rank, 0), axis=0)
    dest = index ^ owner_me
    hit = (mine[None, None, :] == dest[:, None, None]) & (mine_rank[None, None, :] == jnp.arange(2)[None, :, None])
    send = jnp.sum(jnp.where(hit, index[None, None, :], 0), axis=2).reshape(-1)
    place = (index ^ owner_me)[:, None] * 2 + rank
    wanted = jnp.arange(frows) * owners + owner_me
    found = maps.reshape(2, -1)[None] == wanted[:, None, None]
    look = jnp.sum(jnp.where(found, place.reshape(2, -1)[None], 0), axis=2)
    here = jnp.sum(found.astype(jnp.int32), axis=2)
    return send.astype(jnp.int32), look.reshape(-1).astype(jnp.int32), here.reshape(-1).astype(jnp.int32)


def exchange_kernel(
    send_ref, look_ref, here_ref, pattern_ref, initial_ref, child_ref,
    front_ref, cols_ref, lead_ref,
    out_buf, in_buf,
    x_send, x_recv, a_send, a_recv, c_send, c_recv, b_send, b_recv, s_send, s_recv, g_send, g_recv,
):
    rows = lax.axis_size("row")
    owners = lax.axis_size("sub") * rows
    depth = lax.axis_size("col") // 2
    frows, tile = initial_ref.shape[0], initial_ref.shape[2]
    half = tile // 2
    sub, row, col = lax.axis_index("sub"), lax.axis_index("row"), lax.axis_index("col")
    me = sub * rows + row
    z, plane = col // 2, col % 2
    other = 1 - plane

    def peer(delta):
        there = me ^ delta
        return (there // rows, there % rows, col)

    up = (sub, row, ((z + 1) % depth) * 2 + plane)
    down = (sub, row, ((z + depth - 1) % depth) * 2 + plane)
    across = (sub, row, z * 2 + other)
    ways = (up, down)

    barrier = pltpu.get_barrier_semaphore()
    for delta in range(1, owners):
        pl.semaphore_signal(barrier, inc=1, device_id=peer(delta), device_id_type=MESH)
    for there in (up, down, across):
        pl.semaphore_signal(barrier, inc=1, device_id=there, device_id_type=MESH)

    for s in range(2):
        out_buf[s] = child_ref[0, 0, send_ref[s]]

    def fill(delta, carry):
        for s in range(2):
            out_buf[delta * 2 + s] = child_ref[0, 0, send_ref[delta * 2 + s]]
        return carry

    lax.fori_loop(1, owners, fill, 0)
    for s in range(2):
        in_buf[s] = out_buf[s]
    pl.semaphore_wait(barrier, owners - 1 + 3)

    def x_copy(delta):
        part = pl.ds(delta * 2, 2)
        return pltpu.make_async_remote_copy(
            src_ref=out_buf.at[part], dst_ref=in_buf.at[part], send_sem=x_send.at[delta],
            recv_sem=x_recv.at[delta], device_id=peer(delta), device_id_type=MESH,
        )

    for delta in range(1, owners):
        x_copy(delta).start()
    for delta in range(1, owners):
        x_copy(delta).wait_recv()

    def assemble(m, carry):
        value = initial_ref[m, 0] * pattern_ref[m].astype(jnp.float32)
        for c in range(2):
            tile_in = in_buf[look_ref[m * 2 + c]]
            value = value + jnp.where(here_ref[m * 2 + c] > 0, tile_in, 0.0)
        front_ref[m] = value

        @pl.when(z == 0)
        def _():
            cols_ref[plane, m] = value

        return carry

    lax.fori_loop(0, frows, assemble, 0)

    quarter = half // 2

    def a_copy(h, i):
        part = cols_ref.at[plane, i // 2, pl.ds(h * half + (i % 2) * quarter, quarter)]
        return pltpu.make_async_remote_copy(
            src_ref=part, dst_ref=part, send_sem=a_send.at[h, i], recv_sem=a_recv.at[h, i],
            device_id=ways[h], device_id_type=MESH,
        )

    hops = (z, (depth - z) % depth)

    def a_step(step, carry):
        for h in range(2):
            i = step - hops[h]
            live = (i >= 0) & (i < 2 * frows)

            @pl.when(live & (z != 0))
            def _():
                a_copy(h, i).wait_recv()

            @pl.when(live & (hops[h] != depth - 1))
            def _():
                a_copy(h, i).start()

        return carry

    lax.fori_loop(0, 2 * frows + depth - 1, a_step, 0)

    piece = half // depth
    group = frows // 2

    def cut(k, h, g, origin):
        return cols_ref.at[k, pl.ds(g * group, group), pl.ds(h * half + origin * piece, piece)]

    def c_copy(k, h, g):
        part = cut(k, h, g, z)
        return pltpu.make_async_remote_copy(
            src_ref=part, dst_ref=part, send_sem=c_send.at[h, g], recv_sem=c_recv.at[h, g],
            device_id=across, device_id_type=MESH,
        )

    for g in range(2):
        for h in range(2):
            c_copy(plane, h, g).start()

    def b_copy(h, g, t, origin):
        part = cut(other, h, g, origin)
        return pltpu.make_async_remote_copy(
            src_ref=part, dst_ref=part, send_sem=b_send.at[h, g, t], recv_sem=b_recv.at[h, g, t],
            device_id=ways[h], device_id_type=MESH,
        )

    def origin_of(h, t):
        return (z + depth - t) % depth if h == 0 else (z + t) % depth

    for g in range(2):
        for h in range(2):
            c_copy(other, h, g).wait_recv()
            b_copy(h, g, 0, origin_of(h, 0)).start()

    def b_step(t, carry):
        for g in range(2):
            for h in range(2):
                b_copy(h, g, t - 1, origin_of(h, t)).wait_recv()

                @pl.when(t < depth - 1)
                def _():
                    b_copy(h, g, t, origin_of(h, t)).start()

        return carry

    lax.fori_loop(1, depth, b_step, 0)

    strip = tile // owners
    sources = (0, 1, col % owners)

    def s_copy(s, delta):
        rows_there = pl.ds((me ^ delta) * strip, strip)
        return pltpu.make_async_remote_copy(
            src_ref=cols_ref.at[:, 0, rows_there], dst_ref=lead_ref.at[s, :, rows_there],
            send_sem=s_send.at[s, delta], recv_sem=s_recv.at[s], device_id=peer(delta), device_id_type=MESH,
        )

    for s, source in enumerate(sources):
        @pl.when(me == source)
        def _():
            for delta in range(1, owners):
                s_copy(s, delta).start()
            mine = pl.ds(pl.multiple_of(me * strip, strip), strip)
            lead_ref[s, :, mine] = cols_ref[:, 0, mine]

    def s_arrival(s):
        mine = pl.ds(me * strip, strip)
        return pltpu.make_async_remote_copy(
            src_ref=cols_ref.at[:, 0, mine], dst_ref=lead_ref.at[s, :, mine],
            send_sem=s_send.at[s, 0], recv_sem=s_recv.at[s], device_id=across, device_id_type=MESH,
        )

    for s, source in enumerate(sources):
        @pl.when(me != source)
        def _():
            s_arrival(s).wait_recv()

    def g_copy(delta, holder):
        part = lead_ref.at[:, :, pl.ds(holder * strip, strip)]
        return pltpu.make_async_remote_copy(
            src_ref=part, dst_ref=part, send_sem=g_send.at[delta], recv_sem=g_recv.at[delta],
            device_id=peer(delta), device_id_type=MESH,
        )

    for delta in range(1, owners):
        g_copy(delta, me).start()
    for delta in range(1, owners):
        g_copy(delta, me ^ delta).wait_recv()

    for delta in range(1, owners):
        g_copy(delta, me).wait_send()
        x_copy(delta).wait_send()
    for s, source in enumerate(sources):
        @pl.when(me == source)
        def _():
            for delta in range(1, owners):
                s_copy(s, delta).wait_send()
    for g in range(2):
        for h in range(2):
            c_copy(plane, h, g).wait_send()

    def b_end(t, carry):
        for g in range(2):
            for h in range(2):
                b_copy(h, g, t, origin_of(h, t)).wait_send()
        return carry

    lax.fori_loop(0, depth - 1, b_end, 0)

    def a_end(i, carry):
        for h in range(2):
            @pl.when(hops[h] != depth - 1)
            def _():
                a_copy(h, i).wait_send()
        return carry

    lax.fori_loop(0, 2 * frows, a_end, 0)


def exchange(initial, pattern, rmap, child_update):
    owners = lax.axis_size("sub") * lax.axis_size("row")
    depth = lax.axis_size("col") // 2
    frows, _, tile, _ = initial.shape
    me = lax.axis_index(("sub", "row"))
    send, look, here = tables(rmap, me, frows)
    smem = pl.BlockSpec(memory_space=pltpu.SMEM)
    vmem = pl.BlockSpec(memory_space=pltpu.VMEM)
    dma = pltpu.SemaphoreType.DMA
    return pl.pallas_call(
        exchange_kernel,
        out_shape=(
            jax.ShapeDtypeStruct((frows, tile, tile), jnp.float32),
            jax.ShapeDtypeStruct((2, frows, tile, tile), jnp.float32),
            jax.ShapeDtypeStruct((3, 2, tile, tile), jnp.float32),
        ),
        in_specs=[smem] * 4 + [vmem] * 2,
        out_specs=(vmem, vmem, vmem),
        scratch_shapes=[
            pltpu.VMEM((2 * owners, tile, tile), jnp.float32),
            pltpu.VMEM((2 * owners, tile, tile), jnp.float32),
            dma((owners,)), dma((owners,)),
            dma((2, 2 * frows)), dma((2, 2 * frows)),
            dma((2, 2)), dma((2, 2)),
            dma((2, 2, depth)), dma((2, 2, depth)),
            dma((3, owners)), dma((3,)),
            dma((owners,)), dma((owners,)),
        ],
        compiler_params=pltpu.CompilerParams(
            collective_id=1, has_side_effects=True, vmem_limit_bytes=56 * MIB
        ),
    )(send, look, here, pattern.reshape(-1), initial, child_update)


def mul(a, b):
    return jnp.dot(a, b, preferred_element_type=jnp.float32, precision=HIGHEST)


def mul_t(a, b):
    return lax.dot_general(
        a, b, (((1,), (1,)), ((), ())), preferred_element_type=jnp.float32, precision=HIGHEST
    )


def factor_block(block, beside=None):
    n = block.shape[0]
    width = 16
    row_id = lax.broadcasted_iota(jnp.int32, (n, n), 0)
    lane_id = lax.broadcasted_iota(jnp.int32, (n, n), 1)
    eye = row_id == lane_id

    def body(step, carry):
        left, right = carry
        if beside is not None:
            beside(step)
        live = row_id < n - width * step
        for i in range(0, width, 2):
            c0 = jnp.broadcast_to(left[:, i:i + 1], (n, n))
            c1 = jnp.broadcast_to(left[:, i + 1:i + 2], (n, n))
            a, b, c = c0[i:i + 1], c0[i + 1:i + 2], c1[i + 1:i + 2]
            ratio = b / a
            inv = 1.0 / (c - b * ratio)
            below = (row_id > i + 1) & live
            g1 = (c1 - c0 * ratio) * inv
            g0 = jnp.where(below, c0 / a - g1 * ratio, jnp.where(row_id == i + 1, ratio, 0.0))
            g1 = jnp.where(below, g1, 0.0)
            left, right = (
                left - g0 * left[i:i + 1] - g1 * left[i + 1:i + 2],
                right - g0 * right[i:i + 1] - g1 * right[i + 1:i + 2],
            )
        left = pltpu.roll(jnp.concatenate([left[width:], left[:width]], axis=0), n - width, 1)
        right = jnp.concatenate([right[width:], right[:width]], axis=0)
        return left, right

    upper, inverse = lax.fori_loop(0, n // width, body, (block, eye.astype(jnp.float32)))
    scale = lax.rsqrt(jnp.sum(jnp.where(eye, upper, 0.0), axis=1, keepdims=True))
    return jnp.where(row_id <= lane_id, upper * scale, 0.0).T, inverse * scale


def factor_tile(tile_value, factor_ref, inverse_ref, beside=(None, None)):
    n = tile_value.shape[0]
    h = n // 2
    sym = 0.5 * (tile_value + tile_value.T)
    l0, t0 = factor_block(sym[:h, :h], beside[0])
    l10 = mul_t(sym[h:, :h], t0)
    l1, t1 = factor_block(sym[h:, h:] - mul_t(l10, l10), beside[1])
    zero = jnp.zeros((h, h), jnp.float32)
    factor_ref[:h, :h] = l0
    factor_ref[:h, h:] = zero
    factor_ref[h:, :h] = l10
    factor_ref[h:, h:] = l1
    inverse_ref[:h, :h] = t0
    inverse_ref[:h, h:] = zero
    inverse_ref[h:, :h] = -mul(t1, mul(l10, t0))
    inverse_ref[h:, h:] = t1


def split(x):
    high = x.astype(jnp.bfloat16)
    return high, (x - high.astype(jnp.float32)).astype(jnp.bfloat16)


def finish_kernel(front_ref, cols_ref, lead_ref, out_ref, f0_ref, i0_ref, f1_ref, i1_ref, own_ref):
    rows = lax.axis_size("row")
    frows, tile = front_ref.shape[0], front_ref.shape[1]
    me = lax.axis_index("sub") * rows + lax.axis_index("row")
    col = lax.axis_index("col")
    eye = (
        lax.broadcasted_iota(jnp.int32, (tile, tile), 0) == lax.broadcasted_iota(jnp.int32, (tile, tile), 1)
    ).astype(jnp.float32)

    factor_tile(lead_ref[0, 0], f0_ref, i0_ref)
    i0 = i0_ref[...]
    l10 = mul_t(lead_ref[1, 0], i0)
    factor_tile(lead_ref[1, 1] - mul_t(l10, l10), f1_ref, i1_ref)
    i1 = i1_ref[...]
    p0 = mul_t(lead_ref[2, 0], i0)
    own_ref[...] = p0
    p1 = mul_t(lead_ref[2, 1] - mul_t(p0, l10), i1)
    p0 = jnp.where(col == 0, eye, jnp.where(col == 1, 0.0, p0))
    p1 = jnp.where(col == 0, 0.0, jnp.where(col == 1, eye, p1))
    n1 = mul(p1, i1)
    n0 = mul(p0 - mul(n1, l10), i0)
    sign = jnp.where(col < 2, 1.0, -1.0)
    keep = jnp.where(col < 2, 0.0, 1.0)
    n0_high, n0_low = split(n0)
    n1_high, n1_low = split(n1)

    def dot_t(a, b):
        return lax.dot_general(a, b, (((1,), (1,)), ((), ())), preferred_element_type=jnp.float32)

    def body(m, carry):
        a0_high, a0_low = split(cols_ref[0, m])
        a1_high, a1_low = split(cols_ref[1, m])
        total = dot_t(a0_low, n0_high) + dot_t(a0_high, n0_low) + dot_t(a1_low, n1_high) + dot_t(a1_high, n1_low)
        total = total + dot_t(a0_high, n0_high) + dot_t(a1_high, n1_high)
        out_ref[m] = keep * front_ref[m] + sign * total
        return carry

    lax.fori_loop(0, frows, body, 0)

    @pl.when(me == 0)
    def _():
        out_ref[0] = jnp.where(col == 0, f0_ref[...], jnp.where(col == 1, 0.0, front_ref[0]))

    @pl.when((me == 1) & (col == 1))
    def _():
        out_ref[0] = f1_ref[...]

    @pl.when((me == 1) & (col > 1))
    def _():
        out_ref[0] = front_ref[0] - mul_t(mul_t(lead_ref[1, 0], i0_ref[...]), own_ref[...])


def finish(front, cols, lead):
    frows, tile, _ = front.shape
    vmem = pl.BlockSpec(memory_space=pltpu.VMEM)
    return pl.pallas_call(
        finish_kernel,
        out_shape=jax.ShapeDtypeStruct(front.shape, jnp.float32),
        in_specs=[vmem] * 3,
        out_specs=vmem,
        scratch_shapes=[pltpu.VMEM((tile, tile), jnp.float32)] * 5,
        compiler_params=pltpu.CompilerParams(vmem_limit_bytes=48 * MIB),
    )(front, cols, lead)


EXTRA = 2
SLABS = 4
RETURNED = 2
LAG = 6


def fast_tables(rmap, me, frows):
    owners = rmap.shape[2]
    maps = rmap.reshape(-1, owners)
    target = maps % owners
    index = jnp.arange(owners)
    before = index[None, None, :] < index[None, :, None]
    rank = jnp.sum(((target[:, None, :] == target[:, :, None]) & before).astype(jnp.int32), axis=2)
    over = rank > 0
    order = jnp.sum((over[:, None, :] & before).astype(jnp.int32), axis=2)
    flat_target, flat_over = target.reshape(-1), over.reshape(-1)
    flat = jnp.arange(owners * owners)
    seat = jnp.sum(
        (
            (flat_target[None, :] == flat_target[:, None]) & flat_over[None, :] & (flat[None, :] < flat[:, None])
        ).astype(jnp.int32),
        axis=1,
    ).reshape(owners, owners)
    fits = jnp.max(jnp.where(over, seat, 0)) < EXTRA

    own = (index == me)[:, None]
    mine = jnp.sum(jnp.where(own, target, 0), axis=0)
    mine_over = jnp.any(own & over, axis=0)
    mine_order = jnp.sum(jnp.where(own, order, 0), axis=0)
    mine_map = jnp.sum(jnp.where(own, maps, 0), axis=0)
    base_hit = (mine[None, :] == (index ^ me)[:, None]) & ~mine_over[None, :]
    base = jnp.sum(jnp.where(base_hit, index[None, :], 0), axis=1)
    over_hit = mine_over[None, :] & (mine_order[None, :] == jnp.arange(2)[:, None])
    over_index = jnp.sum(jnp.where(over_hit, index[None, :], 0), axis=1)
    near = (index ^ me)[:, None]
    spot = (near * 2 + order).reshape(-1)
    relay_hit = (
        flat_over[None, None, :]
        & (flat_target[None, None, :] == (index ^ me)[:, None, None])
        & (seat.reshape(-1)[None, None, :] == jnp.arange(EXTRA)[None, :, None])
    )
    relay = jnp.sum(jnp.where(relay_hit, spot[None, None, :], 0), axis=2).reshape(-1)
    place = jnp.where(over, owners + seat, near)
    wanted = jnp.arange(frows) * owners + me
    found = maps.reshape(2, -1)[None] == wanted[:, None, None]
    look = jnp.sum(jnp.where(found, place.reshape(2, -1)[None], 0), axis=2).reshape(-1)
    here = jnp.sum(found.astype(jnp.int32), axis=2).reshape(-1)
    lead_hit = mine_map[None, :] == jnp.arange(2)[:, None]
    lead_index = jnp.sum(jnp.where(lead_hit, index[None, :], 0), axis=1)
    lead_here = jnp.sum(lead_hit.astype(jnp.int32), axis=1)
    table = jnp.concatenate([base, over_index, relay, lead_index, lead_here, look, here]).astype(jnp.int32)
    return table, fits


def fast_kernel(
    table_ref, pattern_ref, initial_ref, child_ref, out_ref,
    out_buf, in_0, in_1, in_2, in_3, over_in, over_src, over_mid, over_out, lead_part, lead_in, lead_strip, lead, cols, own_row,
    f0_ref, i0_ref, f1_ref, i1_ref, p0_ref,
    x_send, x_recv, o_send, o_recv, w_send, w_recv, l_send, l_recv, b_send, b_recv, g_send, g_recv,
    a_send, a_recv, c_send, c_recv, d_send, d_recv, r_send, r_recv, h_send, h_recv,
):
    rows = lax.axis_size("row")
    owners = lax.axis_size("sub") * rows
    columns = lax.axis_size("col")
    depth = columns // 2
    frows, tile = initial_ref.shape[0], initial_ref.shape[2]
    half, strip, slab = tile // 2, tile // owners, tile // SLABS
    in_slabs = (in_0, in_1, in_2, in_3)
    sub, row, col = lax.axis_index("sub"), lax.axis_index("row"), lax.axis_index("col")
    me = sub * rows + row
    z, plane = col // 2, col % 2
    other = 1 - plane

    base_at, over_at = 0, owners
    relay_at = over_at + 2
    lead_at = relay_at + owners * EXTRA
    lead_here_at = lead_at + 2
    look_at = lead_here_at + 2
    here_at = look_at + 2 * frows

    def peer(delta):
        there = me ^ delta
        return (there // rows, there % rows, col)

    def line(delta):
        return (sub, row, col ^ delta)

    ways = ((sub, row, ((z + 1) % depth) * 2 + plane), (sub, row, ((z + depth - 1) % depth) * 2 + plane))

    def push(src, dst, send, recv, there):
        return pltpu.make_async_remote_copy(
            src_ref=src, dst_ref=dst, send_sem=send, recv_sem=recv, device_id=there, device_id_type=MESH
        )

    def strip_of(owner):
        return pl.ds(pl.multiple_of(owner * strip, strip), strip)

    def l_copy(delta):
        return push(
            lead_part.at[:, strip_of(me ^ delta)], lead_in.at[delta], l_send.at[delta], l_recv.at[delta], peer(delta)
        )

    def o_copy(delta):
        return push(
            over_src.at[:, strip_of(me ^ delta)], over_mid.at[pl.ds(2 * delta, 2)],
            o_send.at[delta], o_recv.at[delta], peer(delta),
        )

    def w_copy(delta, holder):
        return push(
            over_out.at[delta], over_in.at[:, strip_of(holder)],
            w_send.at[delta], w_recv.at[delta], peer(delta),
        )

    def x_copy(delta, c):
        part = pl.ds(c * slab, slab)
        return push(
            out_buf.at[delta, part], in_slabs[c].at[delta], x_send.at[c, delta], x_recv.at[c, delta], peer(delta)
        )

    def b_copy(delta, k):
        return push(lead_strip, lead.at[k, :, strip_of(me)], b_send.at[delta], b_recv.at[k], line(delta))

    def g_copy(delta, holder):
        part = lead.at[:, :, strip_of(holder)]
        return push(part, part, g_send.at[delta], g_recv.at[delta], peer(delta))

    barrier = pltpu.get_barrier_semaphore()
    for delta in range(1, owners):
        pl.semaphore_signal(barrier, inc=1, device_id=peer(delta), device_id_type=MESH)
    for delta in range(1, columns):
        pl.semaphore_signal(barrier, inc=1, device_id=line(delta), device_id_type=MESH)

    @pl.when(z == 0)
    def _():
        for p in range(2):
            value = jnp.where(table_ref[lead_here_at + p] > 0, child_ref[0, 0, table_ref[lead_at + p]], 0.0)
            first = initial_ref[0, 0] * pattern_ref[0].astype(jnp.float32)
            lead_part[p] = value + jnp.where(me == p, first, 0.0)

    for s in range(2):
        over_src[s] = child_ref[0, 0, table_ref[over_at + s]]

    def fill(delta, carry):
        out_buf[delta] = child_ref[0, 0, table_ref[base_at + delta]]
        return carry

    lax.fori_loop(1, owners, fill, 0)
    for c in range(SLABS):
        in_slabs[c][0] = child_ref[0, 0, table_ref[base_at], pl.ds(c * slab, slab)]
    pl.semaphore_wait(barrier, owners - 1 + columns - 1)

    everyone = range(1, owners)
    @pl.when(z == 0)
    def _():
        for delta in everyone:
            l_copy(delta).start()

    for delta in everyone:
        o_copy(delta).start()
    for delta in everyone:
        x_copy(delta, 0).start()

    @pl.when(z == 0)
    def _():
        total = lead_part[:, strip_of(me)]
        for delta in everyone:
            l_copy(delta).wait_recv()
            total = total + lead_in[delta]
        lead_strip[...] = total
        lead[plane, :, strip_of(me)] = total
        for delta in range(1, columns):
            b_copy(delta, plane).start()

    for delta in everyone:
        o_copy(delta).wait_recv()
    for s in range(2):
        over_mid[s] = over_src[s, strip_of(me)]

    def relay(delta, carry):
        for e in range(EXTRA):
            over_out[delta, e] = over_mid[table_ref[relay_at + delta * EXTRA + e]]
        return carry

    lax.fori_loop(0, owners, relay, 0)
    for e in range(EXTRA):
        over_in[e, strip_of(me)] = over_out[0, e]
    for delta in everyone:
        w_copy(delta, me).start()
    for delta in everyone:
        x_copy(delta, 1).start()
    for k in range(2):
        @pl.when(col != k)
        def _():
            b_copy(0, k).wait_recv()
    for delta in everyone:
        g_copy(delta, me).start()
    for c in range(2, SLABS):
        for delta in everyone:
            x_copy(delta, c).start()

    def slab_arrives(c):
        for delta in everyone:
            x_copy(delta, c).wait_recv()
            if c == 0:
                w_copy(delta, me ^ delta).wait_recv()

    def assembled_slab(m, c):
        part = pl.ds(c * slab, slab)
        value = initial_ref[m, 0, part] * pattern_ref[m].astype(jnp.float32)
        for child in range(2):
            spot = table_ref[look_at + m * 2 + child]
            direct = in_slabs[c][jnp.minimum(spot, owners - 1)]
            relayed = over_in[jnp.maximum(spot - owners, 0), part]
            tile_in = jnp.where(spot < owners, direct, relayed)
            value = value + jnp.where(table_ref[here_at + m * 2 + child] > 0, tile_in, 0.0)
        return value

    def assembled(m):
        return jnp.concatenate([assembled_slab(m, c) for c in range(SLABS)], axis=0)

    def each(start, stop, do):
        def body(i, carry):
            do(i)
            return carry

        lax.fori_loop(start, stop, body, 0)

    def root_slab(c):
        slab_arrives(c)
        part = pl.ds(c * slab, slab)

        def fill_column(m):
            cols[plane, m, part] = assembled_slab(m, c)

        each(0, frows, fill_column)

    units = SLABS * frows
    turn = depth // 2
    feeds = (z < turn, (z == 0) | (z > turn + 1))

    def unit(k, i):
        third = i < 3 * frows + 1
        lead_unit = i < 2 * frows + 2
        c = jnp.where(i < 2 * frows, i // frows, jnp.where(lead_unit, i - 2 * frows + 2, jnp.where(third, 2, 3)))
        m = jnp.where(
            i < 2 * frows, i % frows,
            jnp.where(lead_unit, 0, jnp.where(third, i - 2 * frows - 1, i - 3 * frows)),
        )
        return cols.at[k, m, pl.ds(pl.multiple_of(c * slab, slab), slab)]

    def a_copy(h, i):
        part = unit(plane, i)
        return push(part, part, a_send.at[h, i], a_recv.at[i], ways[h])

    def c_copy(k, i):
        part = unit(k, i)
        return push(part, part, c_send.at[i], c_recv.at[i], line(1))

    def d_copy(h, i):
        part = unit(other, i)
        return push(part, part, d_send.at[h, i], d_recv.at[i], ways[h])

    def bridge(i):
        return turn + i % 2

    def returns(i):
        return (i < RETURNED * frows) & (i % frows != 0)

    def crosses(i):
        return jnp.logical_not(returns(i)) | (z == bridge(i))

    def goes(i):
        up = ((z > turn) & (z < depth - 1)) | ((z == turn) & (bridge(i) == turn))
        down = ((z >= 1) & (z <= turn)) | ((z == turn + 1) & (bridge(i) == turn + 1))
        return up, down

    behinds = (
        4 + LAG * jnp.abs(z - turn),
        jnp.where(z > turn, 4 + LAG * (z - turn - 1), 5 + LAG * (turn - z)),
    )

    def d_step(i):
        @pl.when(z == bridge(i))
        def _():
            c_copy(other, i).wait_recv()

        @pl.when(z != bridge(i))
        def _():
            d_copy(0, i).wait_recv()

        for h, goes_on in enumerate(goes(i)):
            @pl.when(goes_on)
            def _():
                d_copy(h, i).start()

    def a_step(i):
        @pl.when(z != 0)
        def _():
            a_copy(0, i).wait_recv()

        for h in range(2):
            @pl.when(feeds[h])
            def _():
                a_copy(h, i).start()

        @pl.when(crosses(i))
        def _():
            c_copy(plane, i).start()

        way_back(i)

    def way_back(i):
        for odd, behind in enumerate(behinds):
            back = i - behind

            @pl.when((back >= 0) & (back % 2 == odd) & returns(back))
            def _():
                d_step(back)

    turns = half // 16
    ahead = units - 4 * turns

    def gate(c, ready):
        @pl.when(ready & (z == 0))
        def _():
            root_slab(c)

    def beside(block):
        def do(step):
            i = ahead + block * turns + step
            for c, first in ((2, 2 * frows), (3, 2 * frows + 1)):
                if ahead + block * turns <= first < ahead + (block + 1) * turns:
                    gate(c, i == first)
            a_step(i)

        return do

    gate(0, True)
    each(0, frows, a_step)
    gate(1, True)
    each(frows, ahead, a_step)
    for delta in everyone:
        g_copy(delta, me ^ delta).wait_recv()
    factor_tile(lead[0, 0], f0_ref, i0_ref, (beside(0), beside(1)))

    early = (0, frows, 2 * frows, 2 * frows + 1)
    for i in early:
        c_copy(1 - plane, i).wait_recv()

    def r_copy(delta):
        there = strip_of(me ^ delta)
        return push(cols.at[:, 0, there], own_row.at[:, there], r_send.at[delta], r_recv.at[0], peer(delta))

    @pl.when(me == col)
    def _():
        for delta in everyone:
            r_copy(delta).start()
        own_row[:, strip_of(me)] = cols[:, 0, strip_of(me)]

    i0 = i0_ref[...]
    l10 = mul_t(lead[0, 1], i0)

    def h_copy(delta, holder):
        part = own_row.at[:, strip_of(holder)]
        return push(part, part, h_send.at[delta], h_recv.at[delta], peer(delta))

    def spread_row(step):
        @pl.when(step == 0)
        def _():
            @pl.when(me != col)
            def _():
                mine = strip_of(me)
                push(
                    cols.at[:, 0, mine], own_row.at[:, mine], r_send.at[0], r_recv.at[0], line(1)
                ).wait_recv()

            for delta in everyone:
                h_copy(delta, me).start()

        beside(3)(step)

    factor_tile(lead[1, 1] - mul_t(l10, l10), f1_ref, i1_ref, (beside(2), spread_row))
    each(units, RETURNED * frows + 6 + LAG * turn, way_back)
    for delta in everyone:
        h_copy(delta, me ^ delta).wait_recv()

    eye = (
        lax.broadcasted_iota(jnp.int32, (tile, tile), 0) == lax.broadcasted_iota(jnp.int32, (tile, tile), 1)
    ).astype(jnp.float32)
    i1 = i1_ref[...]
    p0 = mul_t(own_row[0], i0)
    p0_ref[...] = p0
    p1 = mul_t(own_row[1] - mul_t(p0, l10), i1)
    p0 = jnp.where(col == 0, eye, jnp.where(col == 1, 0.0, p0))
    p1 = jnp.where(col == 0, 0.0, jnp.where(col == 1, eye, p1))
    n1 = mul(p1, i1)
    n0 = mul(p0 - mul(n1, l10), i0)
    sign = jnp.where(col < 2, 1.0, -1.0)
    keep = jnp.where(col < 2, 0.0, 1.0)
    n0_high, n0_low = split(n0)
    n1_high, n1_low = split(n1)

    @pl.when(z != 0)
    def _():
        for c in range(SLABS):
            slab_arrives(c)

    def dot_t(a, b):
        return lax.dot_general(a, b, (((1,), (1,)), ((), ())), preferred_element_type=jnp.float32)

    def update(m):
        a0_high, a0_low = split(cols[0, m])
        a1_high, a1_low = split(cols[1, m])
        total = dot_t(a0_low, n0_high) + dot_t(a0_high, n0_low) + dot_t(a1_low, n1_high) + dot_t(a1_high, n1_low)
        total = total + dot_t(a0_high, n0_high) + dot_t(a1_high, n1_high)
        out_ref[m] = keep * assembled(m) + sign * total

    def last(m):
        for start in (2 * frows + 1, 3 * frows):
            c_copy(other, start + m).wait_recv()
        update(m)

    update(0)
    each(1, frows, last)

    @pl.when(me == 0)
    def _():
        out_ref[0] = jnp.where(col == 0, f0_ref[...], jnp.where(col == 1, 0.0, assembled(0)))

    @pl.when((me == 1) & (col == 1))
    def _():
        out_ref[0] = f1_ref[...]

    @pl.when((me == 1) & (col > 1))
    def _():
        out_ref[0] = assembled(0) - mul_t(l10, p0_ref[...])

    @pl.when(z == 0)
    def _():
        for delta in everyone:
            l_copy(delta).wait_send()
        for delta in range(1, columns):
            b_copy(delta, plane).wait_send()

    for delta in everyone:
        o_copy(delta).wait_send()
        w_copy(delta, me).wait_send()
        for c in range(SLABS):
            x_copy(delta, c).wait_send()
        g_copy(delta, me).wait_send()
        h_copy(delta, me).wait_send()

    @pl.when(me == col)
    def _():
        for delta in everyone:
            r_copy(delta).wait_send()

    def sent(i):
        for h in range(2):
            @pl.when(feeds[h])
            def _():
                a_copy(h, i).wait_send()

        @pl.when(crosses(i))
        def _():
            c_copy(plane, i).wait_send()

        for h, goes_on in enumerate(goes(i)):
            @pl.when(goes_on & returns(i))
            def _():
                d_copy(h, i).wait_send()

    each(0, units, sent)


def fast(table, pattern, initial, child_update):
    owners = lax.axis_size("sub") * lax.axis_size("row")
    columns = lax.axis_size("col")
    frows, _, tile, _ = initial.shape
    strip, units = tile // owners, SLABS * frows
    smem = pl.BlockSpec(memory_space=pltpu.SMEM)
    vmem = pl.BlockSpec(memory_space=pltpu.VMEM)
    dma = pltpu.SemaphoreType.DMA

    def room(*shape):
        return pltpu.VMEM(shape, jnp.float32)

    return pl.pallas_call(
        fast_kernel,
        out_shape=jax.ShapeDtypeStruct((frows, tile, tile), jnp.float32),
        in_specs=[smem] * 2 + [vmem] * 2,
        out_specs=vmem,
        scratch_shapes=[
            room(owners, tile, tile), *[room(owners, tile // SLABS, tile)] * SLABS, room(EXTRA, tile, tile),
            room(2, tile, tile), room(2 * owners, strip, tile), room(owners, EXTRA, strip, tile),
            room(2, tile, tile), room(owners, 2, strip, tile), room(2, strip, tile), room(2, 2, tile, tile),
            room(2, frows, tile, tile), room(2, tile, tile),
        ] + [room(tile, tile)] * 5 + [
            dma((SLABS, owners)), dma((SLABS, owners)), dma((owners,)), dma((owners,)), dma((owners,)), dma((owners,)),
            dma((owners,)), dma((owners,)), dma((columns,)), dma((2,)), dma((owners,)), dma((owners,)),
            dma((2, units)), dma((units,)), dma((units,)), dma((units,)), dma((2, units)), dma((units,)),
            dma((owners,)), dma((1,)), dma((owners,)), dma((owners,)),
        ],
        compiler_params=pltpu.CompilerParams(
            collective_id=0, has_side_effects=True, vmem_limit_bytes=56 * MIB
        ),
    )(table, pattern.reshape(-1), initial, child_update)


def general(table, pattern, initial, child_update, rmap):
    return finish(*exchange(initial, pattern, rmap, child_update))


def per_device(initial, pattern, rmap, child_update):
    me = lax.axis_index(("sub", "row"))
    table, fits = fast_tables(rmap, me, initial.shape[0])
    out = lax.cond(
        fits,
        lambda table, pattern, initial, child_update, rmap: fast(table, pattern, initial, child_update),
        general,
        table, pattern, initial, child_update, rmap,
    )
    return out[:, None]


def solution(mesh):
    return jax.shard_map(
        per_device,
        mesh=mesh,
        in_specs=(
            P(None, ("sub", "row"), None, "col"),
            P(None, ("sub", "row"), "col"),
            P(),
            P("sub", "row", None, None, "col"),
        ),
        out_specs=P(None, ("sub", "row"), None, "col"),
        check_vma=False,
    )
```

```python
import functools

import jax
import jax.numpy as jnp
from jax import lax
from jax.experimental import pallas as pl
from jax.experimental.pallas import tpu as pltpu
from jax.sharding import PartitionSpec as P

MESH = pl.DeviceIdType.MESH
MIB = 1024 * 1024
HIGHEST = lax.Precision.HIGHEST


def tables(rmap, owner_me, frows):
    owners = rmap.shape[2]
    maps = rmap.reshape(-1, owners)
    target = maps % owners
    index = jnp.arange(owners)
    earlier = (target[:, None, :] == target[:, :, None]) & (index[None, None, :] < index[None, :, None])
    rank = jnp.sum(earlier.astype(jnp.int32), axis=2)
    mine = jnp.sum(jnp.where((index == owner_me)[:, None], target, 0), axis=0)
    mine_rank = jnp.sum(jnp.where((index == owner_me)[:, None], rank, 0), axis=0)
    dest = index ^ owner_me
    hit = (mine[None, None, :] == dest[:, None, None]) & (mine_rank[None, None, :] == jnp.arange(2)[None, :, None])
    send = jnp.sum(jnp.where(hit, index[None, None, :], 0), axis=2).reshape(-1)
    place = (index ^ owner_me)[:, None] * 2 + rank
    wanted = jnp.arange(frows) * owners + owner_me
    found = maps.reshape(2, -1)[None] == wanted[:, None, None]
    look = jnp.sum(jnp.where(found, place.reshape(2, -1)[None], 0), axis=2)
    here = jnp.sum(found.astype(jnp.int32), axis=2)
    return send.astype(jnp.int32), look.reshape(-1).astype(jnp.int32), here.reshape(-1).astype(jnp.int32)


def exchange_kernel(
    send_ref, look_ref, here_ref, pattern_ref, initial_ref, child_ref,
    front_ref, cols_ref, lead_ref,
    out_buf, in_buf,
    x_send, x_recv, a_send, a_recv, c_send, c_recv, b_send, b_recv, s_send, s_recv, g_send, g_recv,
):
    rows = lax.axis_size("row")
    owners = lax.axis_size("sub") * rows
    depth = lax.axis_size("col") // 2
    frows, tile = initial_ref.shape[0], initial_ref.shape[2]
    half = tile // 2
    sub, row, col = lax.axis_index("sub"), lax.axis_index("row"), lax.axis_index("col")
    me = sub * rows + row
    z, plane = col // 2, col % 2
    other = 1 - plane

    def peer(delta):
        there = me ^ delta
        return (there // rows, there % rows, col)

    up = (sub, row, ((z + 1) % depth) * 2 + plane)
    down = (sub, row, ((z + depth - 1) % depth) * 2 + plane)
    across = (sub, row, z * 2 + other)
    ways = (up, down)

    barrier = pltpu.get_barrier_semaphore()
    for delta in range(1, owners):
        pl.semaphore_signal(barrier, inc=1, device_id=peer(delta), device_id_type=MESH)
    for there in (up, down, across):
        pl.semaphore_signal(barrier, inc=1, device_id=there, device_id_type=MESH)

    for s in range(2):
        out_buf[s] = child_ref[0, 0, send_ref[s]]

    def fill(delta, carry):
        for s in range(2):
            out_buf[delta * 2 + s] = child_ref[0, 0, send_ref[delta * 2 + s]]
        return carry

    lax.fori_loop(1, owners, fill, 0)
    for s in range(2):
        in_buf[s] = out_buf[s]
    pl.semaphore_wait(barrier, owners - 1 + 3)

    def x_copy(delta):
        part = pl.ds(delta * 2, 2)
        return pltpu.make_async_remote_copy(
            src_ref=out_buf.at[part], dst_ref=in_buf.at[part], send_sem=x_send.at[delta],
            recv_sem=x_recv.at[delta], device_id=peer(delta), device_id_type=MESH,
        )

    for delta in range(1, owners):
        x_copy(delta).start()
    for delta in range(1, owners):
        x_copy(delta).wait_recv()

    def assemble(m, carry):
        value = initial_ref[m, 0] * pattern_ref[m].astype(jnp.float32)
        for c in range(2):
            tile_in = in_buf[look_ref[m * 2 + c]]
            value = value + jnp.where(here_ref[m * 2 + c] > 0, tile_in, 0.0)
        front_ref[m] = value

        @pl.when(z == 0)
        def _():
            cols_ref[plane, m] = value

        return carry

    lax.fori_loop(0, frows, assemble, 0)

    quarter = half // 2

    def a_copy(h, i):
        part = cols_ref.at[plane, i // 2, pl.ds(h * half + (i % 2) * quarter, quarter)]
        return pltpu.make_async_remote_copy(
            src_ref=part, dst_ref=part, send_sem=a_send.at[h, i], recv_sem=a_recv.at[h, i],
            device_id=ways[h], device_id_type=MESH,
        )

    hops = (z, (depth - z) % depth)

    def a_step(step, carry):
        for h in range(2):
            i = step - hops[h]
            live = (i >= 0) & (i < 2 * frows)

            @pl.when(live & (z != 0))
            def _():
                a_copy(h, i).wait_recv()

            @pl.when(live & (hops[h] != depth - 1))
            def _():
                a_copy(h, i).start()

        return carry

    lax.fori_loop(0, 2 * frows + depth - 1, a_step, 0)

    piece = half // depth
    group = frows // 2

    def cut(k, h, g, origin):
        return cols_ref.at[k, pl.ds(g * group, group), pl.ds(h * half + origin * piece, piece)]

    def c_copy(k, h, g):
        part = cut(k, h, g, z)
        return pltpu.make_async_remote_copy(
            src_ref=part, dst_ref=part, send_sem=c_send.at[h, g], recv_sem=c_recv.at[h, g],
            device_id=across, device_id_type=MESH,
        )

    for g in range(2):
        for h in range(2):
            c_copy(plane, h, g).start()

    def b_copy(h, g, t, origin):
        part = cut(other, h, g, origin)
        return pltpu.make_async_remote_copy(
            src_ref=part, dst_ref=part, send_sem=b_send.at[h, g, t], recv_sem=b_recv.at[h, g, t],
            device_id=ways[h], device_id_type=MESH,
        )

    def origin_of(h, t):
        return (z + depth - t) % depth if h == 0 else (z + t) % depth

    for g in range(2):
        for h in range(2):
            c_copy(other, h, g).wait_recv()
            b_copy(h, g, 0, origin_of(h, 0)).start()

    def b_step(t, carry):
        for g in range(2):
            for h in range(2):
                b_copy(h, g, t - 1, origin_of(h, t)).wait_recv()

                @pl.when(t < depth - 1)
                def _():
                    b_copy(h, g, t, origin_of(h, t)).start()

        return carry

    lax.fori_loop(1, depth, b_step, 0)

    strip = tile // owners
    sources = (0, 1, col % owners)

    def s_copy(s, delta):
        rows_there = pl.ds((me ^ delta) * strip, strip)
        return pltpu.make_async_remote_copy(
            src_ref=cols_ref.at[:, 0, rows_there], dst_ref=lead_ref.at[s, :, rows_there],
            send_sem=s_send.at[s, delta], recv_sem=s_recv.at[s], device_id=peer(delta), device_id_type=MESH,
        )

    for s, source in enumerate(sources):
        @pl.when(me == source)
        def _():
            for delta in range(1, owners):
                s_copy(s, delta).start()
            mine = pl.ds(pl.multiple_of(me * strip, strip), strip)
            lead_ref[s, :, mine] = cols_ref[:, 0, mine]

    def s_arrival(s):
        mine = pl.ds(me * strip, strip)
        return pltpu.make_async_remote_copy(
            src_ref=cols_ref.at[:, 0, mine], dst_ref=lead_ref.at[s, :, mine],
            send_sem=s_send.at[s, 0], recv_sem=s_recv.at[s], device_id=across, device_id_type=MESH,
        )

    for s, source in enumerate(sources):
        @pl.when(me != source)
        def _():
            s_arrival(s).wait_recv()

    def g_copy(delta, holder):
        part = lead_ref.at[:, :, pl.ds(holder * strip, strip)]
        return pltpu.make_async_remote_copy(
            src_ref=part, dst_ref=part, send_sem=g_send.at[delta], recv_sem=g_recv.at[delta],
            device_id=peer(delta), device_id_type=MESH,
        )

    for delta in range(1, owners):
        g_copy(delta, me).start()
    for delta in range(1, owners):
        g_copy(delta, me ^ delta).wait_recv()

    for delta in range(1, owners):
        g_copy(delta, me).wait_send()
        x_copy(delta).wait_send()
    for s, source in enumerate(sources):
        @pl.when(me == source)
        def _():
            for delta in range(1, owners):
                s_copy(s, delta).wait_send()
    for g in range(2):
        for h in range(2):
            c_copy(plane, h, g).wait_send()

    def b_end(t, carry):
        for g in range(2):
            for h in range(2):
                b_copy(h, g, t, origin_of(h, t)).wait_send()
        return carry

    lax.fori_loop(0, depth - 1, b_end, 0)

    def a_end(i, carry):
        for h in range(2):
            @pl.when(hops[h] != depth - 1)
            def _():
                a_copy(h, i).wait_send()
        return carry

    lax.fori_loop(0, 2 * frows, a_end, 0)


def exchange(initial, pattern, rmap, child_update):
    owners = lax.axis_size("sub") * lax.axis_size("row")
    depth = lax.axis_size("col") // 2
    frows, _, tile, _ = initial.shape
    me = lax.axis_index(("sub", "row"))
    send, look, here = tables(rmap, me, frows)
    smem = pl.BlockSpec(memory_space=pltpu.SMEM)
    vmem = pl.BlockSpec(memory_space=pltpu.VMEM)
    dma = pltpu.SemaphoreType.DMA
    return pl.pallas_call(
        exchange_kernel,
        out_shape=(
            jax.ShapeDtypeStruct((frows, tile, tile), jnp.float32),
            jax.ShapeDtypeStruct((2, frows, tile, tile), jnp.float32),
            jax.ShapeDtypeStruct((3, 2, tile, tile), jnp.float32),
        ),
        in_specs=[smem] * 4 + [vmem] * 2,
        out_specs=(vmem, vmem, vmem),
        scratch_shapes=[
            pltpu.VMEM((2 * owners, tile, tile), jnp.float32),
            pltpu.VMEM((2 * owners, tile, tile), jnp.float32),
            dma((owners,)), dma((owners,)),
            dma((2, 2 * frows)), dma((2, 2 * frows)),
            dma((2, 2)), dma((2, 2)),
            dma((2, 2, depth)), dma((2, 2, depth)),
            dma((3, owners)), dma((3,)),
            dma((owners,)), dma((owners,)),
        ],
        compiler_params=pltpu.CompilerParams(
            collective_id=1, has_side_effects=True, vmem_limit_bytes=56 * MIB
        ),
    )(send, look, here, pattern.reshape(-1), initial, child_update)


def mul(a, b):
    return jnp.dot(a, b, preferred_element_type=jnp.float32, precision=HIGHEST)


def mul_t(a, b):
    return lax.dot_general(
        a, b, (((1,), (1,)), ((), ())), preferred_element_type=jnp.float32, precision=HIGHEST
    )


def factor_block(block, beside=None):
    n = block.shape[0]
    width = 16
    row_id = lax.broadcasted_iota(jnp.int32, (n, n), 0)
    lane_id = lax.broadcasted_iota(jnp.int32, (n, n), 1)
    eye = row_id == lane_id

    def body(step, carry):
        left, right = carry
        if beside is not None:
            beside(step)
        live = row_id < n - width * step
        for i in range(0, width, 2):
            c0 = jnp.broadcast_to(left[:, i:i + 1], (n, n))
            c1 = jnp.broadcast_to(left[:, i + 1:i + 2], (n, n))
            a, b, c = c0[i:i + 1], c0[i + 1:i + 2], c1[i + 1:i + 2]
            ratio = b / a
            inv = 1.0 / (c - b * ratio)
            below = (row_id > i + 1) & live
            g1 = (c1 - c0 * ratio) * inv
            g0 = jnp.where(below, c0 / a - g1 * ratio, jnp.where(row_id == i + 1, ratio, 0.0))
            g1 = jnp.where(below, g1, 0.0)
            left, right = (
                left - g0 * left[i:i + 1] - g1 * left[i + 1:i + 2],
                right - g0 * right[i:i + 1] - g1 * right[i + 1:i + 2],
            )
        left = pltpu.roll(jnp.concatenate([left[width:], left[:width]], axis=0), n - width, 1)
        right = jnp.concatenate([right[width:], right[:width]], axis=0)
        return left, right

    upper, inverse = lax.fori_loop(0, n // width, body, (block, eye.astype(jnp.float32)))
    scale = lax.rsqrt(jnp.sum(jnp.where(eye, upper, 0.0), axis=1, keepdims=True))
    return jnp.where(row_id <= lane_id, upper * scale, 0.0).T, inverse * scale


def factor_tile(tile_value, factor_ref, inverse_ref, beside=(None, None)):
    n = tile_value.shape[0]
    h = n // 2
    sym = 0.5 * (tile_value + tile_value.T)
    l0, t0 = factor_block(sym[:h, :h], beside[0])
    l10 = mul_t(sym[h:, :h], t0)
    l1, t1 = factor_block(sym[h:, h:] - mul_t(l10, l10), beside[1])
    zero = jnp.zeros((h, h), jnp.float32)
    factor_ref[:h, :h] = l0
    factor_ref[:h, h:] = zero
    factor_ref[h:, :h] = l10
    factor_ref[h:, h:] = l1
    inverse_ref[:h, :h] = t0
    inverse_ref[:h, h:] = zero
    inverse_ref[h:, :h] = -mul(t1, mul(l10, t0))
    inverse_ref[h:, h:] = t1


def split(x):
    high = x.astype(jnp.bfloat16)
    return high, (x - high.astype(jnp.float32)).astype(jnp.bfloat16)


def finish_kernel(front_ref, cols_ref, lead_ref, out_ref, f0_ref, i0_ref, f1_ref, i1_ref, own_ref):
    rows = lax.axis_size("row")
    frows, tile = front_ref.shape[0], front_ref.shape[1]
    me = lax.axis_index("sub") * rows + lax.axis_index("row")
    col = lax.axis_index("col")
    eye = (
        lax.broadcasted_iota(jnp.int32, (tile, tile), 0) == lax.broadcasted_iota(jnp.int32, (tile, tile), 1)
    ).astype(jnp.float32)

    factor_tile(lead_ref[0, 0], f0_ref, i0_ref)
    i0 = i0_ref[...]
    l10 = mul_t(lead_ref[1, 0], i0)
    factor_tile(lead_ref[1, 1] - mul_t(l10, l10), f1_ref, i1_ref)
    i1 = i1_ref[...]
    p0 = mul_t(lead_ref[2, 0], i0)
    own_ref[...] = p0
    p1 = mul_t(lead_ref[2, 1] - mul_t(p0, l10), i1)
    p0 = jnp.where(col == 0, eye, jnp.where(col == 1, 0.0, p0))
    p1 = jnp.where(col == 0, 0.0, jnp.where(col == 1, eye, p1))
    n1 = mul(p1, i1)
    n0 = mul(p0 - mul(n1, l10), i0)
    sign = jnp.where(col < 2, 1.0, -1.0)
    keep = jnp.where(col < 2, 0.0, 1.0)
    n0_high, n0_low = split(n0)
    n1_high, n1_low = split(n1)

    def dot_t(a, b):
        return lax.dot_general(a, b, (((1,), (1,)), ((), ())), preferred_element_type=jnp.float32)

    def body(m, carry):
        a0_high, a0_low = split(cols_ref[0, m])
        a1_high, a1_low = split(cols_ref[1, m])
        total = dot_t(a0_low, n0_high) + dot_t(a0_high, n0_low) + dot_t(a1_low, n1_high) + dot_t(a1_high, n1_low)
        total = total + dot_t(a0_high, n0_high) + dot_t(a1_high, n1_high)
        out_ref[m] = keep * front_ref[m] + sign * total
        return carry

    lax.fori_loop(0, frows, body, 0)

    @pl.when(me == 0)
    def _():
        out_ref[0] = jnp.where(col == 0, f0_ref[...], jnp.where(col == 1, 0.0, front_ref[0]))

    @pl.when((me == 1) & (col == 1))
    def _():
        out_ref[0] = f1_ref[...]

    @pl.when((me == 1) & (col > 1))
    def _():
        out_ref[0] = front_ref[0] - mul_t(mul_t(lead_ref[1, 0], i0_ref[...]), own_ref[...])


def finish(front, cols, lead):
    frows, tile, _ = front.shape
    vmem = pl.BlockSpec(memory_space=pltpu.VMEM)
    return pl.pallas_call(
        finish_kernel,
        out_shape=jax.ShapeDtypeStruct(front.shape, jnp.float32),
        in_specs=[vmem] * 3,
        out_specs=vmem,
        scratch_shapes=[pltpu.VMEM((tile, tile), jnp.float32)] * 5,
        compiler_params=pltpu.CompilerParams(vmem_limit_bytes=48 * MIB),
    )(front, cols, lead)


EXTRA = 2
SLABS = 4
RETURNED = 2
LAG = 8


def fast_tables(rmap, me, frows):
    owners = rmap.shape[2]
    maps = rmap.reshape(-1, owners)
    target = maps % owners
    index = jnp.arange(owners)
    before = index[None, None, :] < index[None, :, None]
    rank = jnp.sum(((target[:, None, :] == target[:, :, None]) & before).astype(jnp.int32), axis=2)
    over = rank > 0
    order = jnp.sum((over[:, None, :] & before).astype(jnp.int32), axis=2)
    flat_target, flat_over = target.reshape(-1), over.reshape(-1)
    flat = jnp.arange(owners * owners)
    seat = jnp.sum(
        (
            (flat_target[None, :] == flat_target[:, None]) & flat_over[None, :] & (flat[None, :] < flat[:, None])
        ).astype(jnp.int32),
        axis=1,
    ).reshape(owners, owners)
    fits = jnp.max(jnp.where(over, seat, 0)) < EXTRA

    own = (index == me)[:, None]
    mine = jnp.sum(jnp.where(own, target, 0), axis=0)
    mine_over = jnp.any(own & over, axis=0)
    mine_order = jnp.sum(jnp.where(own, order, 0), axis=0)
    mine_map = jnp.sum(jnp.where(own, maps, 0), axis=0)
    base_hit = (mine[None, :] == (index ^ me)[:, None]) & ~mine_over[None, :]
    base = jnp.sum(jnp.where(base_hit, index[None, :], 0), axis=1)
    over_hit = mine_over[None, :] & (mine_order[None, :] == jnp.arange(2)[:, None])
    over_index = jnp.sum(jnp.where(over_hit, index[None, :], 0), axis=1)
    near = (index ^ me)[:, None]
    spot = (near * 2 + order).reshape(-1)
    relay_hit = (
        flat_over[None, None, :]
        & (flat_target[None, None, :] == (index ^ me)[:, None, None])
        & (seat.reshape(-1)[None, None, :] == jnp.arange(EXTRA)[None, :, None])
    )
    relay = jnp.sum(jnp.where(relay_hit, spot[None, None, :], 0), axis=2).reshape(-1)
    place = jnp.where(over, owners + seat, near)
    wanted = jnp.arange(frows) * owners + me
    found = maps.reshape(2, -1)[None] == wanted[:, None, None]
    look = jnp.sum(jnp.where(found, place.reshape(2, -1)[None], 0), axis=2).reshape(-1)
    here = jnp.sum(found.astype(jnp.int32), axis=2).reshape(-1)
    lead_hit = mine_map[None, :] == jnp.arange(2)[:, None]
    lead_index = jnp.sum(jnp.where(lead_hit, index[None, :], 0), axis=1)
    lead_here = jnp.sum(lead_hit.astype(jnp.int32), axis=1)
    table = jnp.concatenate([base, over_index, relay, lead_index, lead_here, look, here]).astype(jnp.int32)
    return table, fits


def fast_kernel(
    table_ref, pattern_ref, initial_ref, child_ref, out_ref,
    out_buf, in_0, in_1, in_2, in_3, over_in, over_src, over_mid, over_out, lead_part, lead_in, lead_strip, lead, cols, own_row,
    f0_ref, i0_ref, f1_ref, i1_ref, p0_ref,
    x_send, x_recv, o_send, o_recv, w_send, w_recv, l_send, l_recv, b_send, b_recv, g_send, g_recv,
    a_send, a_recv, c_send, c_recv, d_send, d_recv, r_send, r_recv, h_send, h_recv,
):
    rows = lax.axis_size("row")
    owners = lax.axis_size("sub") * rows
    columns = lax.axis_size("col")
    depth = columns // 2
    frows, tile = initial_ref.shape[0], initial_ref.shape[2]
    half, strip, slab = tile // 2, tile // owners, tile // SLABS
    in_slabs = (in_0, in_1, in_2, in_3)
    sub, row, col = lax.axis_index("sub"), lax.axis_index("row"), lax.axis_index("col")
    me = sub * rows + row
    z, plane = col // 2, col % 2
    other = 1 - plane

    base_at, over_at = 0, owners
    relay_at = over_at + 2
    lead_at = relay_at + owners * EXTRA
    lead_here_at = lead_at + 2
    look_at = lead_here_at + 2
    here_at = look_at + 2 * frows

    def peer(delta):
        there = me ^ delta
        return (there // rows, there % rows, col)

    def line(delta):
        return (sub, row, col ^ delta)

    ways = ((sub, row, ((z + 1) % depth) * 2 + plane), (sub, row, ((z + depth - 1) % depth) * 2 + plane))

    def push(src, dst, send, recv, there):
        return pltpu.make_async_remote_copy(
            src_ref=src, dst_ref=dst, send_sem=send, recv_sem=recv, device_id=there, device_id_type=MESH
        )

    def strip_of(owner):
        return pl.ds(pl.multiple_of(owner * strip, strip), strip)

    def l_copy(delta):
        return push(
            lead_part.at[:, strip_of(me ^ delta)], lead_in.at[delta], l_send.at[delta], l_recv.at[delta], peer(delta)
        )

    def o_copy(delta):
        return push(
            over_src.at[:, strip_of(me ^ delta)], over_mid.at[pl.ds(2 * delta, 2)],
            o_send.at[delta], o_recv.at[delta], peer(delta),
        )

    def w_copy(delta, holder):
        return push(
            over_out.at[delta], over_in.at[:, strip_of(holder)],
            w_send.at[delta], w_recv.at[delta], peer(delta),
        )

    def x_copy(delta, c):
        part = pl.ds(c * slab, slab)
        return push(
            out_buf.at[delta, part], in_slabs[c].at[delta], x_send.at[c, delta], x_recv.at[c, delta], peer(delta)
        )

    def b_copy(delta, k):
        return push(lead_strip, lead.at[k, :, strip_of(me)], b_send.at[delta], b_recv.at[k], line(delta))

    def g_copy(delta, holder):
        part = lead.at[:, :, strip_of(holder)]
        return push(part, part, g_send.at[delta], g_recv.at[delta], peer(delta))

    barrier = pltpu.get_barrier_semaphore()
    for delta in range(1, owners):
        pl.semaphore_signal(barrier, inc=1, device_id=peer(delta), device_id_type=MESH)
    for delta in range(1, columns):
        pl.semaphore_signal(barrier, inc=1, device_id=line(delta), device_id_type=MESH)

    @pl.when(z == 0)
    def _():
        for p in range(2):
            value = jnp.where(table_ref[lead_here_at + p] > 0, child_ref[0, 0, table_ref[lead_at + p]], 0.0)
            first = initial_ref[0, 0] * pattern_ref[0].astype(jnp.float32)
            lead_part[p] = value + jnp.where(me == p, first, 0.0)

    for s in range(2):
        over_src[s] = child_ref[0, 0, table_ref[over_at + s]]

    def fill(delta, carry):
        out_buf[delta] = child_ref[0, 0, table_ref[base_at + delta]]
        return carry

    lax.fori_loop(1, owners, fill, 0)
    for c in range(SLABS):
        in_slabs[c][0] = child_ref[0, 0, table_ref[base_at], pl.ds(c * slab, slab)]
    pl.semaphore_wait(barrier, owners - 1 + columns - 1)

    everyone = range(1, owners)
    @pl.when(z == 0)
    def _():
        for delta in everyone:
            l_copy(delta).start()

    for delta in everyone:
        o_copy(delta).start()
    for delta in everyone:
        x_copy(delta, 0).start()

    @pl.when(z == 0)
    def _():
        total = lead_part[:, strip_of(me)]
        for delta in everyone:
            l_copy(delta).wait_recv()
            total = total + lead_in[delta]
        lead_strip[...] = total
        lead[plane, :, strip_of(me)] = total
        for delta in range(1, columns):
            b_copy(delta, plane).start()

    for delta in everyone:
        o_copy(delta).wait_recv()
    for s in range(2):
        over_mid[s] = over_src[s, strip_of(me)]

    def relay(delta, carry):
        for e in range(EXTRA):
            over_out[delta, e] = over_mid[table_ref[relay_at + delta * EXTRA + e]]
        return carry

    lax.fori_loop(0, owners, relay, 0)
    for e in range(EXTRA):
        over_in[e, strip_of(me)] = over_out[0, e]
    for delta in everyone:
        w_copy(delta, me).start()
    for delta in everyone:
        x_copy(delta, 1).start()
    for k in range(2):
        @pl.when(col != k)
        def _():
            b_copy(0, k).wait_recv()
    for delta in everyone:
        g_copy(delta, me).start()
    for c in range(2, SLABS):
        for delta in everyone:
            x_copy(delta, c).start()

    def slab_arrives(c):
        for delta in everyone:
            x_copy(delta, c).wait_recv()
            if c == 0:
                w_copy(delta, me ^ delta).wait_recv()

    def assembled_slab(m, c):
        part = pl.ds(c * slab, slab)
        value = initial_ref[m, 0, part] * pattern_ref[m].astype(jnp.float32)
        for child in range(2):
            spot = table_ref[look_at + m * 2 + child]
            direct = in_slabs[c][jnp.minimum(spot, owners - 1)]
            relayed = over_in[jnp.maximum(spot - owners, 0), part]
            tile_in = jnp.where(spot < owners, direct, relayed)
            value = value + jnp.where(table_ref[here_at + m * 2 + child] > 0, tile_in, 0.0)
        return value

    def assembled(m):
        return jnp.concatenate([assembled_slab(m, c) for c in range(SLABS)], axis=0)

    def each(start, stop, do):
        def body(i, carry):
            do(i)
            return carry

        lax.fori_loop(start, stop, body, 0)

    def root_slab(c):
        slab_arrives(c)
        part = pl.ds(c * slab, slab)

        def fill_column(m):
            cols[plane, m, part] = assembled_slab(m, c)

        each(0, frows, fill_column)

    units = SLABS * frows
    turn = depth // 2
    feeds = (z < turn, (z == 0) | (z > turn + 1))

    def unit(k, i):
        third = i < 3 * frows + 1
        lead_unit = i < 2 * frows + 2
        c = jnp.where(i < 2 * frows, i // frows, jnp.where(lead_unit, i - 2 * frows + 2, jnp.where(third, 2, 3)))
        m = jnp.where(
            i < 2 * frows, i % frows,
            jnp.where(lead_unit, 0, jnp.where(third, i - 2 * frows - 1, i - 3 * frows)),
        )
        return cols.at[k, m, pl.ds(pl.multiple_of(c * slab, slab), slab)]

    def a_copy(h, i):
        part = unit(plane, i)
        return push(part, part, a_send.at[h, i], a_recv.at[i], ways[h])

    def c_copy(k, i):
        part = unit(k, i)
        return push(part, part, c_send.at[i], c_recv.at[i], line(1))

    def d_copy(h, i):
        part = unit(other, i)
        return push(part, part, d_send.at[h, i], d_recv.at[i], ways[h])

    def bridge(i):
        return turn + i % 2

    def returns(i):
        return (i < RETURNED * frows) & (i % frows != 0)

    def crosses(i):
        return jnp.logical_not(returns(i)) | (z == bridge(i))

    def goes(i):
        up = ((z > turn) & (z < depth - 1)) | ((z == turn) & (bridge(i) == turn))
        down = ((z >= 1) & (z <= turn)) | ((z == turn + 1) & (bridge(i) == turn + 1))
        return up, down

    behinds = (
        4 + LAG * jnp.abs(z - turn),
        jnp.where(z > turn, 4 + LAG * (z - turn - 1), 5 + LAG * (turn - z)),
    )

    def d_step(i):
        @pl.when(z == bridge(i))
        def _():
            c_copy(other, i).wait_recv()

        @pl.when(z != bridge(i))
        def _():
            d_copy(0, i).wait_recv()

        for h, goes_on in enumerate(goes(i)):
            @pl.when(goes_on)
            def _():
                d_copy(h, i).start()

    def a_step(i):
        @pl.when(z != 0)
        def _():
            a_copy(0, i).wait_recv()

        for h in range(2):
            @pl.when(feeds[h])
            def _():
                a_copy(h, i).start()

        @pl.when(crosses(i))
        def _():
            c_copy(plane, i).start()

        way_back(i)

    def way_back(i):
        for odd, behind in enumerate(behinds):
            back = i - behind

            @pl.when((back >= 0) & (back % 2 == odd) & returns(back))
            def _():
                d_step(back)

    turns = half // 16
    ahead = units - 4 * turns

    def gate(c, ready):
        @pl.when(ready & (z == 0))
        def _():
            root_slab(c)

    def beside(block):
        def do(step):
            i = ahead + block * turns + step
            for c, first in ((2, 2 * frows), (3, 2 * frows + 1)):
                if ahead + block * turns <= first < ahead + (block + 1) * turns:
                    gate(c, i == first)
            a_step(i)

        return do

    gate(0, True)
    each(0, frows, a_step)
    gate(1, True)
    each(frows, ahead, a_step)
    for delta in everyone:
        g_copy(delta, me ^ delta).wait_recv()
    factor_tile(lead[0, 0], f0_ref, i0_ref, (beside(0), beside(1)))

    early = (0, frows, 2 * frows, 2 * frows + 1)
    for i in early:
        c_copy(1 - plane, i).wait_recv()

    def r_copy(delta):
        there = strip_of(me ^ delta)
        return push(cols.at[:, 0, there], own_row.at[:, there], r_send.at[delta], r_recv.at[0], peer(delta))

    @pl.when(me == col)
    def _():
        for delta in everyone:
            r_copy(delta).start()
        own_row[:, strip_of(me)] = cols[:, 0, strip_of(me)]

    i0 = i0_ref[...]
    l10 = mul_t(lead[0, 1], i0)

    def h_copy(delta, holder):
        part = own_row.at[:, strip_of(holder)]
        return push(part, part, h_send.at[delta], h_recv.at[delta], peer(delta))

    def spread_row(step):
        @pl.when(step == 0)
        def _():
            @pl.when(me != col)
            def _():
                mine = strip_of(me)
                push(
                    cols.at[:, 0, mine], own_row.at[:, mine], r_send.at[0], r_recv.at[0], line(1)
                ).wait_recv()

            for delta in everyone:
                h_copy(delta, me).start()

        beside(3)(step)

    factor_tile(lead[1, 1] - mul_t(l10, l10), f1_ref, i1_ref, (beside(2), spread_row))
    each(units, RETURNED * frows + 6 + LAG * turn, way_back)
    for delta in everyone:
        h_copy(delta, me ^ delta).wait_recv()

    eye = (
        lax.broadcasted_iota(jnp.int32, (tile, tile), 0) == lax.broadcasted_iota(jnp.int32, (tile, tile), 1)
    ).astype(jnp.float32)
    i1 = i1_ref[...]
    p0 = mul_t(own_row[0], i0)
    p0_ref[...] = p0
    p1 = mul_t(own_row[1] - mul_t(p0, l10), i1)
    p0 = jnp.where(col == 0, eye, jnp.where(col == 1, 0.0, p0))
    p1 = jnp.where(col == 0, 0.0, jnp.where(col == 1, eye, p1))
    n1 = mul(p1, i1)
    n0 = mul(p0 - mul(n1, l10), i0)
    sign = jnp.where(col < 2, 1.0, -1.0)
    keep = jnp.where(col < 2, 0.0, 1.0)
    n0_high, n0_low = split(n0)
    n1_high, n1_low = split(n1)

    @pl.when(z != 0)
    def _():
        for c in range(SLABS):
            slab_arrives(c)

    def dot_t(a, b):
        return lax.dot_general(a, b, (((1,), (1,)), ((), ())), preferred_element_type=jnp.float32)

    def update(m):
        a0_high, a0_low = split(cols[0, m])
        a1_high, a1_low = split(cols[1, m])
        total = dot_t(a0_low, n0_high) + dot_t(a0_high, n0_low) + dot_t(a1_low, n1_high) + dot_t(a1_high, n1_low)
        total = total + dot_t(a0_high, n0_high) + dot_t(a1_high, n1_high)
        out_ref[m] = keep * assembled(m) + sign * total

    def last(m):
        for start in (2 * frows + 1, 3 * frows):
            c_copy(other, start + m).wait_recv()
        update(m)

    update(0)
    each(1, frows, last)

    @pl.when(me == 0)
    def _():
        out_ref[0] = jnp.where(col == 0, f0_ref[...], jnp.where(col == 1, 0.0, assembled(0)))

    @pl.when((me == 1) & (col == 1))
    def _():
        out_ref[0] = f1_ref[...]

    @pl.when((me == 1) & (col > 1))
    def _():
        out_ref[0] = assembled(0) - mul_t(l10, p0_ref[...])

    @pl.when(z == 0)
    def _():
        for delta in everyone:
            l_copy(delta).wait_send()
        for delta in range(1, columns):
            b_copy(delta, plane).wait_send()

    for delta in everyone:
        o_copy(delta).wait_send()
        w_copy(delta, me).wait_send()
        for c in range(SLABS):
            x_copy(delta, c).wait_send()
        g_copy(delta, me).wait_send()
        h_copy(delta, me).wait_send()

    @pl.when(me == col)
    def _():
        for delta in everyone:
            r_copy(delta).wait_send()

    def sent(i):
        for h in range(2):
            @pl.when(feeds[h])
            def _():
                a_copy(h, i).wait_send()

        @pl.when(crosses(i))
        def _():
            c_copy(plane, i).wait_send()

        for h, goes_on in enumerate(goes(i)):
            @pl.when(goes_on & returns(i))
            def _():
                d_copy(h, i).wait_send()

    each(0, units, sent)


def fast(table, pattern, initial, child_update):
    owners = lax.axis_size("sub") * lax.axis_size("row")
    columns = lax.axis_size("col")
    frows, _, tile, _ = initial.shape
    strip, units = tile // owners, SLABS * frows
    smem = pl.BlockSpec(memory_space=pltpu.SMEM)
    vmem = pl.BlockSpec(memory_space=pltpu.VMEM)
    dma = pltpu.SemaphoreType.DMA

    def room(*shape):
        return pltpu.VMEM(shape, jnp.float32)

    return pl.pallas_call(
        fast_kernel,
        out_shape=jax.ShapeDtypeStruct((frows, tile, tile), jnp.float32),
        in_specs=[smem] * 2 + [vmem] * 2,
        out_specs=vmem,
        scratch_shapes=[
            room(owners, tile, tile), *[room(owners, tile // SLABS, tile)] * SLABS, room(EXTRA, tile, tile),
            room(2, tile, tile), room(2 * owners, strip, tile), room(owners, EXTRA, strip, tile),
            room(2, tile, tile), room(owners, 2, strip, tile), room(2, strip, tile), room(2, 2, tile, tile),
            room(2, frows, tile, tile), room(2, tile, tile),
        ] + [room(tile, tile)] * 5 + [
            dma((SLABS, owners)), dma((SLABS, owners)), dma((owners,)), dma((owners,)), dma((owners,)), dma((owners,)),
            dma((owners,)), dma((owners,)), dma((columns,)), dma((2,)), dma((owners,)), dma((owners,)),
            dma((2, units)), dma((units,)), dma((units,)), dma((units,)), dma((2, units)), dma((units,)),
            dma((owners,)), dma((1,)), dma((owners,)), dma((owners,)),
        ],
        compiler_params=pltpu.CompilerParams(
            collective_id=0, has_side_effects=True, vmem_limit_bytes=56 * MIB
        ),
    )(table, pattern.reshape(-1), initial, child_update)


def general(table, pattern, initial, child_update, rmap):
    return finish(*exchange(initial, pattern, rmap, child_update))


def per_device(initial, pattern, rmap, child_update):
    me = lax.axis_index(("sub", "row"))
    table, fits = fast_tables(rmap, me, initial.shape[0])
    out = lax.cond(
        fits,
        lambda table, pattern, initial, child_update, rmap: fast(table, pattern, initial, child_update),
        general,
        table, pattern, initial, child_update, rmap,
    )
    return out[:, None]


def solution(mesh):
    return jax.shard_map(
        per_device,
        mesh=mesh,
        in_specs=(
            P(None, ("sub", "row"), None, "col"),
            P(None, ("sub", "row"), "col"),
            P(),
            P("sub", "row", None, None, "col"),
        ),
        out_specs=P(None, ("sub", "row"), None, "col"),
        check_vma=False,
    )
```
